32 devices in a mesh: head: 4 (over z), ctx: 8 (over y, x, core).
Axes of the slice: x: 2, y: 2, z: 4, core: 2. Of those that a mesh axis runs over, the one named last changes fastest.
Arguments:
- queries: bfloat16 [2048, 3584], P(('head', 'ctx')), may hold values from -6 to 6
- keys: bfloat16 [2048, 512], P(('head', 'ctx')), may hold values from -12 to 12
- values: bfloat16 [2048, 512], P(('head', 'ctx')), may hold values from -6 to 6
- block_index: int32 [16, 28, 16], replicated, may hold values from 0 to 15, as said below
- block_count: int32 [16, 28], replicated, may hold values from 1 to 16, as said below
- head_order: int32 [28], replicated, may hold values from 0 to 27, as said below
Outputs:
- attention_out: bfloat16 [2048, 3584], P(('head', 'ctx'))
The draws below stay inside these ranges and needn't reach their ends.
Inputs may be any that keep to these rules, and one draw needn't show every extreme that they name: For query block b and head h the first block_count[b, h] entries of block_index[b, h] are distinct key blocks in ascending order, always including block 0 and block b and never above b; the later entries name the remaining blocks. block_count[b, h] is at most b + 1. `head_order`: A permutation of the 28 query heads; each aligned block of 7 entries that starts at a multiple of 7 holds heads of exactly two key and value heads (head // 7).
All inputs are finite; a program needn't handle non-finite values.
Results may differ from the reference program's by a relative error of at most 0.0045.
Values may be sent and summed in bfloat16 or wider, within the bound.
A program may use at most 64 MiB of HBM per device.

```python
import math
import jax
import jax.numpy as jnp
from jax import lax

H = 28
KVH = 4
HD = 128
BLOCK = 128
SEQ = 2048


def head_plan(key):
    per_group = H // KVH
    half_count = KVH // 2
    kv_order = jax.random.permutation(jax.random.fold_in(key, 101), KVH).astype(jnp.int32)
    head_iota = jnp.arange(H, dtype=jnp.int32)
    kv_of = head_iota // per_group
    is_dense = jnp.any(kv_of[:, None] == kv_order[None, :half_count], axis=1)
    strong = jax.random.randint(jax.random.fold_in(key, 102), (H,), 384, 1025)
    sparse = jax.random.randint(jax.random.fold_in(key, 103), (H,), 8, 97)
    chosen = jax.random.randint(jax.random.fold_in(key, 104), (KVH,), 0, per_group)
    full_head = head_iota % per_group == jnp.take(chosen, kv_of)
    limits = jnp.where(is_dense, jnp.where(full_head, 1024, strong), sparse)
    return (kv_order, limits)


def block_plan(key):
    kv_order, limits = head_plan(key)
    blocks = SEQ // BLOCK
    rolled = jax.random.randint(jax.random.fold_in(key, 105), (blocks, H, blocks), 0, 1024)
    query_block = jnp.arange(blocks, dtype=jnp.int32)[:, None, None]
    key_block = jnp.arange(blocks, dtype=jnp.int32)[None, None, :]
    attended = ((rolled < limits[None, :, None]) | (key_block == 0) | (key_block == query_block)) & (key_block <= query_block)
    ranking = jnp.where(attended, key_block, key_block + blocks)
    index_table = jnp.argsort(ranking, axis=-1, stable=True).astype(jnp.int32)
    count_table = jnp.sum(attended.astype(jnp.int32), axis=-1).astype(jnp.int32)
    return (index_table, count_table)


def draw_block_index(key, part):
    index_table, count_table = block_plan(key)
    return index_table


def draw_block_count(key, part):
    index_table, count_table = block_plan(key)
    return count_table


def draw_head_order(key, part):
    kv_order, limits = head_plan(key)
    key = jax.random.fold_in(key, 3)
    per_group = H // KVH
    half_count = KVH // 2
    lane_iota = jnp.arange(per_group, dtype=jnp.int32)
    split_at = jax.random.randint(jax.random.fold_in(key, 1), (half_count,), per_group // 2, per_group // 2 + 2)
    head_lists = []
    for pair_index in range(half_count):
        dense_kv = kv_order[pair_index]
        sparse_kv = kv_order[pair_index + half_count]
        dense_perm = jax.random.permutation(jax.random.fold_in(key, 10 + pair_index), per_group).astype(jnp.int32)
        sparse_perm = jax.random.permutation(jax.random.fold_in(key, 20 + pair_index), per_group).astype(jnp.int32)
        leading = lane_iota < split_at[pair_index]
        list_one = jnp.where(leading, dense_kv * per_group + dense_perm, sparse_kv * per_group + sparse_perm)
        list_two = jnp.where(leading, sparse_kv * per_group + sparse_perm, dense_kv * per_group + dense_perm)
        head_lists.append(list_one)
        head_lists.append(list_two)
    stacked = jnp.stack(head_lists)
    placing = jax.random.permutation(jax.random.fold_in(key, 30), KVH)
    return stacked[placing].reshape(H).astype(jnp.int32)


def draw_queries(key, part):
    key = jax.random.fold_in(key, 4)
    drawn = jnp.clip(jax.random.normal(key, (SEQ, H * HD), jnp.float32), -6.0, 6.0)
    return drawn.astype(jnp.bfloat16)


def draw_keys(key, part):
    key = jax.random.fold_in(key, 5)
    row_scales = jnp.exp(jax.random.uniform(jax.random.fold_in(key, 1), (SEQ, KVH, 1), jnp.float32, math.log(0.3), math.log(3.0)))
    drawn = jnp.clip(jax.random.normal(key, (SEQ, KVH, HD), jnp.float32), -4.0, 4.0) * row_scales
    return drawn.reshape(SEQ, KVH * HD).astype(jnp.bfloat16)


def block_scale(stream_key, shape, split, smallest, largest):
    def one(dim, parts):
        steps = jax.random.uniform(jax.random.fold_in(jax.random.fold_in(stream_key, 6), dim), (parts,), jnp.float32, smallest / len(split), largest / len(split))
        return jnp.repeat(jnp.exp(steps), shape[dim] // parts).reshape((-1,) + (1,) * (len(shape) - dim - 1))

    factor_of = one(*split[0])
    for cut in split[1:]:
        factor_of = factor_of * one(*cut)
    return factor_of


def normal_values(own_key, extent, scale, most, split=(), kind=jnp.bfloat16):
    result = jax.random.normal(own_key, extent, jnp.float32) * scale
    if len(split) > 0:
        result = block_scale(own_key, extent, split, -0.22, 0.18) * result
    return jnp.clip(result, min=-most, max=most).astype(kind)


def setup_inputs(seed: int = 0) -> dict:
    arg_keys = jax.random.split(jax.random.key(seed), 7)
    return {
        "queries": draw_queries(jax.random.fold_in(arg_keys[6], 71), 0),
        "keys": draw_keys(jax.random.fold_in(arg_keys[6], 71), 0),
        "values": normal_values(arg_keys[2], (SEQ, KVH * HD), 1.0, 6.0, ((0, 32),)),
        "block_index": draw_block_index(jax.random.fold_in(arg_keys[6], 71), 0),
        "block_count": draw_block_count(jax.random.fold_in(arg_keys[6], 71), 0),
        "head_order": draw_head_order(jax.random.fold_in(arg_keys[6], 71), 0),
    }


def attend_group(operands):
    query_tile, key_rows, value_rows, allowed = operands
    scores = jnp.einsum('gqd,kd->gqk', query_tile.astype(jnp.float32), key_rows.astype(jnp.float32)) * (1.0 / math.sqrt(HD))
    scores = jnp.where(allowed, scores, -jnp.inf)
    row_top = lax.optimization_barrier(jnp.max(scores, axis=-1, keepdims=True))
    weights = jnp.exp(scores - row_top)
    row_total = lax.optimization_barrier(jnp.sum(weights, axis=-1, keepdims=True))
    rounded = weights.astype(jnp.bfloat16)
    mixed_out = jnp.einsum('gqk,kd->gqd', rounded.astype(jnp.float32), value_rows.astype(jnp.float32))
    return mixed_out / row_total

def reference(queries, keys, values, block_index, block_count, head_order):
    per_group = H // KVH
    tile_rows = min(512, SEQ)
    per_tile = tile_rows // BLOCK
    blocks = SEQ // BLOCK
    query_heads = queries.reshape(SEQ, KVH, per_group, HD).transpose(1, 2, 0, 3)
    key_heads = keys.reshape(SEQ, KVH, HD).transpose(1, 0, 2)
    value_heads = values.reshape(SEQ, KVH, HD).transpose(1, 0, 2)
    block_iota = jnp.arange(blocks, dtype=jnp.int32)
    outputs = []
    for number in range(SEQ // tile_rows):
        length = (number + 1) * tile_rows
        first_row = number * tile_rows
        reach = length // BLOCK
        listed = block_index[number * per_tile:(number + 1) * per_tile]
        counted = block_count[number * per_tile:(number + 1) * per_tile]
        usable = block_iota[None, None, :] < counted[:, :, None]
        block_hits = (listed[:, :, :, None] == block_iota[None, None, None, :]) & usable[:, :, :, None]
        table_flags = jnp.any(block_hits, axis=2)[:, :, :reach]
        table_flags = table_flags.transpose(1, 0, 2).reshape(KVH, per_group, per_tile, 1, reach, 1)
        allowed = jnp.broadcast_to(table_flags, (KVH, per_group, per_tile, BLOCK, reach, BLOCK))
        allowed = allowed.reshape(KVH, per_group, tile_rows, length)
        query_pos = first_row + jnp.arange(tile_rows, dtype=jnp.int32)
        key_pos = jnp.arange(length, dtype=jnp.int32)
        allowed = allowed & (key_pos[None, :] <= query_pos[:, None])[None, None]
        mixed_out = lax.map(attend_group, (query_heads[:, :, first_row:first_row + tile_rows], key_heads[:, :length], value_heads[:, :length], allowed))
        outputs.append(mixed_out)
    attended = jnp.concatenate(outputs, axis=2).reshape(H, SEQ, HD)
    ordered = jnp.take(attended, head_order, axis=0)
    return ordered.transpose(1, 0, 2).reshape(SEQ, H * HD).astype(jnp.bfloat16)
```

```python
from functools import partial
import math

import jax
import jax.numpy as jnp
from jax import lax
from jax.experimental import pallas as pl
from jax.experimental.pallas import tpu as pltpu
from jax.sharding import PartitionSpec as P

H = 28
KVH = 4
HD = 128
BLOCK = 128


FLOOR = -1e30
MESH = pl.DeviceIdType.MESH


def positions(stripes, stripe_len, device, ctx_total):
    offsets = jnp.arange(stripes * stripe_len, dtype=jnp.int32)
    stripe = offsets // stripe_len
    return (stripe * ctx_total + device) * stripe_len + offsets % stripe_len


def keep_state(carried):
    return carried


def update_lanes(query_rows, key_lanes, value_lanes, allowed, score_scale, carried):
    running_max, running_sum, running_out = carried
    scores = (
        jnp.einsum("qgd,kgd->qgk", query_rows, key_lanes, preferred_element_type=jnp.float32)
        * score_scale
    )
    scores = jnp.where(allowed, scores, FLOOR)
    new_max = jnp.maximum(running_max, jnp.max(scores, axis=2))
    weights = jnp.where(allowed, jnp.exp(scores - new_max[:, :, None]), 0.0)
    factor = jnp.exp(running_max - new_max)
    new_sum = running_sum * factor + jnp.sum(weights, axis=2)
    update = jnp.einsum(
        "qgk,kgd->qgd",
        weights.astype(jnp.bfloat16),
        value_lanes,
        preferred_element_type=jnp.float32,
    )
    new_out = running_out * factor[:, :, None] + update
    return (new_max, new_sum, new_out)


def local(queries, keys, values, block_index, block_count, head_order):
    local_tokens = queries.shape[0]
    per_group = H // KVH
    head_total = lax.axis_size("head")
    ctx_total = lax.axis_size("ctx")
    ctx_here = lax.axis_index("ctx")
    head_here = lax.axis_index("head")
    query_split = queries.reshape(local_tokens, H, HD)
    key_split = keys.reshape(local_tokens, KVH, HD)
    value_split = values.reshape(local_tokens, KVH, HD)
    query_sorted = jnp.take(query_split, head_order, axis=1)
    kv_lists = (head_order // per_group).reshape(head_total, per_group)
    kv_pairs = jnp.stack([jnp.min(kv_lists, axis=1), jnp.max(kv_lists, axis=1)], axis=1).reshape(
        head_total * 2
    )
    key_sent = jnp.take(key_split, kv_pairs, axis=1).reshape(local_tokens, head_total, 2, HD)
    value_sent = jnp.take(value_split, kv_pairs, axis=1).reshape(local_tokens, head_total, 2, HD)
    own_heads = lax.dynamic_slice_in_dim(head_order, head_here * per_group, per_group)
    own_kv = own_heads // per_group
    slot_of = (own_kv == jnp.max(own_kv)).astype(jnp.int32)
    query_sent = query_sorted.reshape(local_tokens, head_total, per_group, HD)
    query_got, key_got, value_got = (
        lax.all_to_all(query_sent, "head", split_axis=1, concat_axis=0, tiled=True),
        lax.all_to_all(key_sent, "head", split_axis=1, concat_axis=0, tiled=True),
        lax.all_to_all(value_sent, "head", split_axis=1, concat_axis=0, tiled=True),
    )
    row_count = head_total * local_tokens
    slot_count = key_sent.shape[2]
    query_rows = query_got.reshape(row_count, per_group, HD)
    key_rows = key_got.reshape(row_count, slot_count, HD)
    value_rows = value_got.reshape(row_count, slot_count, HD)
    query_pos = positions(head_total, local_tokens, ctx_here, ctx_total)
    per_entry = min(local_tokens, BLOCK)
    entries = row_count // per_entry
    entry_blocks = query_pos[::per_entry] // BLOCK
    block_total = block_index.shape[2]
    block_iota = jnp.arange(block_total, dtype=jnp.int32)
    listed = jnp.take(jnp.take(block_index, entry_blocks, axis=0), own_heads, axis=1)
    counted = jnp.take(jnp.take(block_count, entry_blocks, axis=0), own_heads, axis=1)
    usable = block_iota[None, None, :] < counted[:, :, None]
    block_hits = (listed[:, :, :, None] == block_iota[None, None, None, :]) & usable[:, :, :, None]
    table_flags = jnp.any(block_hits, axis=2).astype(jnp.bfloat16)
    score_scale = 1.0 / math.sqrt(HD)
    initial = (
        jnp.full((row_count, per_group), FLOOR, jnp.float32),
        jnp.zeros((row_count, per_group), jnp.float32),
        jnp.zeros((row_count, per_group, HD), jnp.float32),
    )
    key_piece = lax.all_gather(key_rows, "ctx", axis=0, tiled=True)
    value_piece = lax.all_gather(value_rows, "ctx", axis=0, tiled=True)
    shard_total = key_piece.shape[0] // row_count

    def one_shard(number, inner_state):
        key_block = lax.dynamic_slice_in_dim(key_piece, number * row_count, row_count, 0)
        value_block = lax.dynamic_slice_in_dim(value_piece, number * row_count, row_count, 0)
        key_lanes = jnp.take(key_block, slot_of, axis=1)
        value_lanes = jnp.take(value_block, slot_of, axis=1)
        key_pos = positions(head_total, local_tokens, number, ctx_total)
        onehot = (block_iota[:, None] == (key_pos // BLOCK)[None, :]).astype(jnp.bfloat16)
        chosen = jnp.einsum("egb,bk->egk", table_flags, onehot, preferred_element_type=jnp.float32)
        spread = jnp.broadcast_to(
            chosen[:, None], (entries, per_entry, per_group, row_count)
        ).reshape(row_count, per_group, row_count)
        allowed = (spread > 0.5) & (key_pos[None, None, :] <= query_pos[:, None, None])
        return lax.cond(
            jnp.any(allowed),
            partial(update_lanes, query_rows, key_lanes, value_lanes, allowed, score_scale),
            keep_state,
            inner_state,
        )

    folded = lax.fori_loop(0, shard_total, one_shard, initial)
    running_max, running_sum, running_out = folded
    attended = (
        (running_out / running_sum[:, :, None])
        .astype(jnp.bfloat16)
        .reshape(row_count, 1, per_group, HD)
    )
    returned = lax.all_to_all(attended, "head", split_axis=0, concat_axis=1, tiled=True).reshape(
        local_tokens, H, HD
    )
    return returned.reshape(local_tokens, H * HD)


LOG2E = 1.4426950408889634
MASKED = -1e30


def plane_kernel(
    q_ref, k_ref, v_ref, table_ref, order_ref, out_ref,
    k_all, v_all, q_in, q_ext, acc, top, total, done, entries,
    local_sems, send_sems, recv_sems,
):
    z = lax.axis_index("head")
    ctx = lax.axis_index("ctx")
    planes = lax.axis_size("head")
    tokens = q_ref.shape[0]
    per_group = H // KVH
    rows = per_group * tokens
    core = ctx % 2
    x_pos = (ctx // 2) % 2
    y_pos = ctx // 4
    sib = ctx + 1 - 2 * core
    xn = ctx + 2 - 4 * x_pos
    yn = ctx + 4 - 8 * y_pos
    dg = xn + 4 - 8 * y_pos
    to_sib = 1 - 2 * core
    query_block = (z * 8 + ctx) * tokens // BLOCK
    bufs = (k_all, v_all)
    heres = (k_ref, v_ref)

    local_copies = [
        pltpu.make_async_copy(q_ref, q_in, local_sems.at[0]),
        pltpu.make_async_copy(table_ref.at[query_block], entries, local_sems.at[1]),
        pltpu.make_async_copy(k_ref, k_all.at[z * 8 + ctx], local_sems.at[2]),
        pltpu.make_async_copy(v_ref, v_all.at[z * 8 + ctx], local_sems.at[3]),
    ]
    for copy in local_copies:
        copy.start()

    barrier = pltpu.get_barrier_semaphore()
    for near in (sib, xn, yn):
        pl.semaphore_signal(
            barrier, inc=1, device_id={"head": z, "ctx": near}, device_id_type=MESH
        )

    @pl.when(z > 0)
    def _():
        pl.semaphore_signal(
            barrier, inc=1, device_id={"head": z - 1, "ctx": ctx}, device_id_type=MESH
        )

    @pl.when(z < planes - 1)
    def _():
        pl.semaphore_signal(
            barrier, inc=1, device_id={"head": z + 1, "ctx": ctx}, device_id_type=MESH
        )

    pl.semaphore_wait(
        barrier, 3 + (z > 0).astype(jnp.int32) + (z < planes - 1).astype(jnp.int32)
    )

    def push(which, k, slot, kind, head_to, ctx_to, own=False):
        place = bufs[which].at[(z - k) * 8 + slot]
        return pltpu.make_async_remote_copy(
            src_ref=heres[which] if own else place,
            dst_ref=place,
            send_sem=send_sems.at[k, kind],
            recv_sem=recv_sems.at[z - k, slot, which],
            device_id={"head": head_to, "ctx": ctx_to},
            device_id_type=MESH,
        )

    def arrived(which, k, slot):
        push(which, k, slot, 0, z, sib).wait_recv()

    def column(k):
        @pl.when(z >= k)
        def _():
            for which in (0, 1):
                if k > 0:
                    arrived(which, k, ctx)

                @pl.when(z < planes - 1)
                def _():
                    push(which, k, ctx, which, z + 1, ctx, k == 0).start()

                push(which, k, ctx, 2 + which, z, xn, k == 0).start()
                push(which, k, ctx, 4 + which, z, yn, k == 0).start()
                push(which, k, ctx, 8 + which, z, sib, k == 0).start()

    def across(k):
        @pl.when(z >= k)
        def _():
            arrived(0, k, xn)
            push(0, k, xn, 6, z, yn).start()
            push(0, k, xn, 10, z, sib).start()
            arrived(1, k, yn)
            push(1, k, yn, 7, z, xn).start()
            push(1, k, yn, 13, z, sib).start()
            arrived(0, k, yn)
            push(0, k, yn, 12, z, sib).start()
            arrived(1, k, xn)
            push(1, k, xn, 11, z, sib).start()

    def corner(k):
        @pl.when(z >= k)
        def _():
            for which in (0, 1):
                arrived(which, k, dg)
                push(which, k, dg, 14 + which, z, sib).start()

    def beside(k):
        @pl.when(z >= k)
        def _():
            for slot in (ctx, xn, yn, dg):
                for which in (0, 1):
                    arrived(which, k, slot + to_sib)

    def sent(k):
        @pl.when(z >= k)
        def _():
            for which in (0, 1):
                @pl.when(z < planes - 1)
                def _():
                    push(which, k, ctx, which, z + 1, ctx).wait_send()
            for kind in range(2, 16):
                push(0, k, ctx, kind, z, sib).wait_send()

    def prepare():
        for copy in local_copies:
            copy.wait()
        listed = entries[...]
        width = listed.shape[1]
        spot = lax.broadcasted_iota(jnp.int32, listed.shape, 1)
        last = jnp.min(jnp.where(listed == query_block, spot, width), axis=1, keepdims=True)
        listed = jnp.where(spot <= last, listed, -1)
        lane = lax.broadcasted_iota(jnp.int32, (H, HD), 1)
        bias = jnp.full((H, HD), MASKED, jnp.float32)
        for e in range(width):
            bias = jnp.where(listed[:, e:e + 1] == lane, 0.0, bias)
        for h in range(H):
            group, row = h // per_group, (h % per_group) * tokens
            q_ext[group, row:row + tokens, :HD] = q_in[:, h * HD:(h + 1) * HD]
            q_ext[group, row:row + tokens, HD:] = jnp.broadcast_to(
                bias[h:h + 1, :], (tokens, HD)
            ).astype(jnp.bfloat16)

    def attend(k):
        @pl.when(z >= k)
        def _():
            plane = z - k
            keys_here = 8 * tokens
            factor = LOG2E / math.sqrt(HD)
            key_row = lax.broadcasted_iota(jnp.int32, (keys_here, HD), 0)
            key_lane = lax.broadcasted_iota(jnp.int32, (keys_here, HD), 1)
            block_of = (plane * keys_here + key_row) // BLOCK
            onehot = jnp.where(block_of == key_lane, 1.0, 0.0).astype(jnp.bfloat16)

            def one_group(j, carry):
                cols = pl.ds(pl.multiple_of(j * HD, HD), HD)
                key = k_all[pl.ds(plane * 8, 8), :, cols].reshape(keys_here, HD)
                value = v_all[pl.ds(plane * 8, 8), :, cols].reshape(keys_here, HD)
                key = jnp.concatenate([key, onehot], axis=1)
                s = lax.dot_general(
                    q_ext[j], key, (((1,), (1,)), ((), ())), preferred_element_type=jnp.float32
                )
                if k == 0:
                    row_pos = ctx * tokens + lax.broadcasted_iota(jnp.int32, s.shape, 0) % tokens
                    col_pos = lax.broadcasted_iota(jnp.int32, s.shape, 1)
                    s = jnp.where(col_pos <= row_pos, s, MASKED)
                high = jnp.max(s, axis=1, keepdims=True)
                if k > 0:
                    old = top[j][:, :1]
                    high = jnp.maximum(high, old)
                    shrink = jnp.exp2((old - high) * factor)
                w = jnp.exp2((s - high) * factor)
                part = w[:, :HD]
                for cut in range(1, keys_here // HD):
                    part = part + w[:, cut * HD:(cut + 1) * HD]
                mixed = jnp.dot(
                    w.astype(jnp.bfloat16), value, preferred_element_type=jnp.float32
                )
                if k > 0:
                    part = part + total[j] * shrink
                    mixed = mixed + acc[j] * shrink
                top[j] = jnp.broadcast_to(high, (rows, HD))
                total[j] = part
                acc[j] = mixed
                return carry

            lax.fori_loop(0, KVH, one_group, 0)

    column(0)
    prepare()
    across(0)
    column(1)
    corner(0)
    for k in range(4):
        if k < 3:
            across(k + 1)
        beside(k)
        if k == 3:
            pass
        attend(k)
        if k < 2:
            column(k + 2)
        if k < 3:
            corner(k + 1)

    def finish(j, carry):
        summed = jnp.sum(total[j], axis=1, keepdims=True)
        done[pl.ds(j * per_group, per_group)] = (
            (acc[j] / summed).astype(jnp.bfloat16).reshape(per_group, tokens, HD)
        )
        return carry

    lax.fori_loop(0, KVH, finish, 0)
    for place in range(H):
        out_ref[:, place * HD:(place + 1) * HD] = done[order_ref[place]]
    for k in range(4):
        sent(k)


def planes_local(queries, keys, values, block_index, block_count, head_order):
    tokens = queries.shape[0]
    planes = lax.axis_size("head")
    rows = H // KVH * tokens
    any_spec = pl.BlockSpec(memory_space=pl.ANY)
    return pl.pallas_call(
        plane_kernel,
        out_shape=jax.ShapeDtypeStruct(queries.shape, jnp.bfloat16),
        in_specs=[any_spec] * 4 + [pl.BlockSpec(memory_space=pltpu.SMEM)],
        out_specs=pl.BlockSpec(memory_space=pltpu.VMEM),
        scratch_shapes=[
            pltpu.VMEM((planes * 8, tokens, KVH * HD), jnp.bfloat16),
            pltpu.VMEM((planes * 8, tokens, KVH * HD), jnp.bfloat16),
            pltpu.VMEM(queries.shape, jnp.bfloat16),
            pltpu.VMEM((KVH, rows, 2 * HD), jnp.bfloat16),
            pltpu.VMEM((KVH, rows, HD), jnp.float32),
            pltpu.VMEM((KVH, rows, HD), jnp.float32),
            pltpu.VMEM((KVH, rows, HD), jnp.float32),
            pltpu.VMEM((H, tokens, HD), jnp.bfloat16),
            pltpu.VMEM(block_index.shape[1:], jnp.int32),
            pltpu.SemaphoreType.DMA((4,)),
            pltpu.SemaphoreType.DMA((planes, 16)),
            pltpu.SemaphoreType.DMA((planes, 8, 2)),
        ],
        compiler_params=pltpu.CompilerParams(
            collective_id=0, has_side_effects=True, vmem_limit_bytes=48 * 1024 * 1024
        ),
    )(queries, keys, values, block_index, head_order)


def solution(mesh):
    in_planes = mesh.shape["head"] == 4 and mesh.shape["ctx"] == 8
    return jax.shard_map(
        planes_local if in_planes else local,
        mesh=mesh,
        in_specs=(
            P(("head", "ctx"), None),
            P(("head", "ctx"), None),
            P(("head", "ctx"), None),
            P(),
            P(),
            P(),
        ),
        out_specs=P(("head", "ctx"), None),
        check_vma=False,
    )
```

```python
from functools import partial
import math

import jax
import jax.numpy as jnp
from jax import lax
from jax.experimental import pallas as pl
from jax.experimental.pallas import tpu as pltpu
from jax.sharding import PartitionSpec as P

H = 28
KVH = 4
HD = 128
BLOCK = 128


FLOOR = -1e30
MESH = pl.DeviceIdType.MESH


def positions(stripes, stripe_len, device, ctx_total):
    offsets = jnp.arange(stripes * stripe_len, dtype=jnp.int32)
    stripe = offsets // stripe_len
    return (stripe * ctx_total + device) * stripe_len + offsets % stripe_len


def keep_state(carried):
    return carried


def update_lanes(query_rows, key_lanes, value_lanes, allowed, score_scale, carried):
    running_max, running_sum, running_out = carried
    scores = (
        jnp.einsum("qgd,kgd->qgk", query_rows, key_lanes, preferred_element_type=jnp.float32)
        * score_scale
    )
    scores = jnp.where(allowed, scores, FLOOR)
    new_max = jnp.maximum(running_max, jnp.max(scores, axis=2))
    weights = jnp.where(allowed, jnp.exp(scores - new_max[:, :, None]), 0.0)
    factor = jnp.exp(running_max - new_max)
    new_sum = running_sum * factor + jnp.sum(weights, axis=2)
    update = jnp.einsum(
        "qgk,kgd->qgd",
        weights.astype(jnp.bfloat16),
        value_lanes,
        preferred_element_type=jnp.float32,
    )
    new_out = running_out * factor[:, :, None] + update
    return (new_max, new_sum, new_out)


def local(queries, keys, values, block_index, block_count, head_order):
    local_tokens = queries.shape[0]
    per_group = H // KVH
    head_total = lax.axis_size("head")
    ctx_total = lax.axis_size("ctx")
    ctx_here = lax.axis_index("ctx")
    head_here = lax.axis_index("head")
    query_split = queries.reshape(local_tokens, H, HD)
    key_split = keys.reshape(local_tokens, KVH, HD)
    value_split = values.reshape(local_tokens, KVH, HD)
    query_sorted = jnp.take(query_split, head_order, axis=1)
    kv_lists = (head_order // per_group).reshape(head_total, per_group)
    kv_pairs = jnp.stack([jnp.min(kv_lists, axis=1), jnp.max(kv_lists, axis=1)], axis=1).reshape(
        head_total * 2
    )
    key_sent = jnp.take(key_split, kv_pairs, axis=1).reshape(local_tokens, head_total, 2, HD)
    value_sent = jnp.take(value_split, kv_pairs, axis=1).reshape(local_tokens, head_total, 2, HD)
    own_heads = lax.dynamic_slice_in_dim(head_order, head_here * per_group, per_group)
    own_kv = own_heads // per_group
    slot_of = (own_kv == jnp.max(own_kv)).astype(jnp.int32)
    query_sent = query_sorted.reshape(local_tokens, head_total, per_group, HD)
    query_got, key_got, value_got = (
        lax.all_to_all(query_sent, "head", split_axis=1, concat_axis=0, tiled=True),
        lax.all_to_all(key_sent, "head", split_axis=1, concat_axis=0, tiled=True),
        lax.all_to_all(value_sent, "head", split_axis=1, concat_axis=0, tiled=True),
    )
    row_count = head_total * local_tokens
    slot_count = key_sent.shape[2]
    query_rows = query_got.reshape(row_count, per_group, HD)
    key_rows = key_got.reshape(row_count, slot_count, HD)
    value_rows = value_got.reshape(row_count, slot_count, HD)
    query_pos = positions(head_total, local_tokens, ctx_here, ctx_total)
    per_entry = min(local_tokens, BLOCK)
    entries = row_count // per_entry
    entry_blocks = query_pos[::per_entry] // BLOCK
    block_total = block_index.shape[2]
    block_iota = jnp.arange(block_total, dtype=jnp.int32)
    listed = jnp.take(jnp.take(block_index, entry_blocks, axis=0), own_heads, axis=1)
    counted = jnp.take(jnp.take(block_count, entry_blocks, axis=0), own_heads, axis=1)
    usable = block_iota[None, None, :] < counted[:, :, None]
    block_hits = (listed[:, :, :, None] == block_iota[None, None, None, :]) & usable[:, :, :, None]
    table_flags = jnp.any(block_hits, axis=2).astype(jnp.bfloat16)
    score_scale = 1.0 / math.sqrt(HD)
    initial = (
        jnp.full((row_count, per_group), FLOOR, jnp.float32),
        jnp.zeros((row_count, per_group), jnp.float32),
        jnp.zeros((row_count, per_group, HD), jnp.float32),
    )
    key_piece = lax.all_gather(key_rows, "ctx", axis=0, tiled=True)
    value_piece = lax.all_gather(value_rows, "ctx", axis=0, tiled=True)
    shard_total = key_piece.shape[0] // row_count

    def one_shard(number, inner_state):
        key_block = lax.dynamic_slice_in_dim(key_piece, number * row_count, row_count, 0)
        value_block = lax.dynamic_slice_in_dim(value_piece, number * row_count, row_count, 0)
        key_lanes = jnp.take(key_block, slot_of, axis=1)
        value_lanes = jnp.take(value_block, slot_of, axis=1)
        key_pos = positions(head_total, local_tokens, number, ctx_total)
        onehot = (block_iota[:, None] == (key_pos // BLOCK)[None, :]).astype(jnp.bfloat16)
        chosen = jnp.einsum("egb,bk->egk", table_flags, onehot, preferred_element_type=jnp.float32)
        spread = jnp.broadcast_to(
            chosen[:, None], (entries, per_entry, per_group, row_count)
        ).reshape(row_count, per_group, row_count)
        allowed = (spread > 0.5) & (key_pos[None, None, :] <= query_pos[:, None, None])
        return lax.cond(
            jnp.any(allowed),
            partial(update_lanes, query_rows, key_lanes, value_lanes, allowed, score_scale),
            keep_state,
            inner_state,
        )

    folded = lax.fori_loop(0, shard_total, one_shard, initial)
    running_max, running_sum, running_out = folded
    attended = (
        (running_out / running_sum[:, :, None])
        .astype(jnp.bfloat16)
        .reshape(row_count, 1, per_group, HD)
    )
    returned = lax.all_to_all(attended, "head", split_axis=0, concat_axis=1, tiled=True).reshape(
        local_tokens, H, HD
    )
    return returned.reshape(local_tokens, H * HD)


LOG2E = 1.4426950408889634
MASKED = -1e30


def plane_kernel(
    q_ref, k_ref, v_ref, table_ref, order_ref, out_ref,
    k_all, v_all, q_in, q_ext, acc, top, total, lists, bias_by_block, bias_by_head,
    done, leaving, local_sems, swap_send, swap_recv, send_sems, recv_sems,
):
    z = lax.axis_index("head")
    ctx = lax.axis_index("ctx")
    planes = lax.axis_size("head")
    tokens = q_ref.shape[0]
    per_group = H // KVH
    groups = KVH // 2
    heads = H // 2
    both = 2 * tokens
    rows = per_group * both
    half = groups * HD
    core = ctx % 2
    other = 1 - core
    chip = ctx // 2
    x_chip = chip + 1 - 2 * (chip % 2)
    y_chip = chip + 2 - 4 * (chip // 2)
    d_chip = x_chip + y_chip - chip
    sib = 2 * chip + other
    query_block = (z * 4 + chip) * both // BLOCK
    bufs = (k_all, v_all)
    heres = (k_ref, v_ref)

    def columns(which_core, width):
        return pl.ds(pl.multiple_of(which_core * width, width), width)

    def token_rows(which_core):
        return pl.ds(pl.multiple_of(which_core * tokens, tokens), tokens)

    local_copies = [
        pltpu.make_async_copy(
            q_ref.at[:, columns(core, heads * HD)], q_in.at[core], local_sems.at[0]
        ),
        pltpu.make_async_copy(table_ref.at[query_block], lists, local_sems.at[1]),
    ]
    for which in (0, 1):
        local_copies.append(pltpu.make_async_copy(
            heres[which].at[:, columns(core, half)],
            bufs[which].at[z * 4 + chip, token_rows(core)],
            local_sems.at[2 + which],
        ))
    for copy in local_copies:
        copy.start()

    barrier = pltpu.get_barrier_semaphore()

    def greet(head_to, ctx_to):
        pl.semaphore_signal(
            barrier, inc=1, device_id={"head": head_to, "ctx": ctx_to}, device_id_type=MESH
        )

    greet(z, sib)
    for which_core in (core, other):
        greet(z, 2 * x_chip + which_core)
        greet(z, 2 * y_chip + which_core)

    @pl.when(z > 0)
    def _():
        greet(z - 1, ctx)
        greet(z - 1, sib)

    @pl.when(z < planes - 1)
    def _():
        greet(z + 1, ctx)
        greet(z + 1, sib)

    pl.semaphore_wait(
        barrier, 5 + 2 * (z > 0).astype(jnp.int32) + 2 * (z < planes - 1).astype(jnp.int32)
    )

    def piece(which, to_core, kind, head_to, ctx_to):
        return pltpu.make_async_remote_copy(
            src_ref=heres[which].at[:, columns(to_core, half)],
            dst_ref=bufs[which].at[z * 4 + chip, token_rows(core)],
            send_sem=send_sems.at[0, kind],
            recv_sem=recv_sems.at[z, chip, which, core],
            device_id={"head": head_to, "ctx": ctx_to},
            device_id_type=MESH,
        )

    def whole(which, k, slot, kind, head_to, ctx_to):
        place = bufs[which].at[(z - k) * 4 + slot]
        return pltpu.make_async_remote_copy(
            src_ref=place,
            dst_ref=place,
            send_sem=send_sems.at[k, kind],
            recv_sem=recv_sems.at[z - k, slot, which, 0],
            device_id={"head": head_to, "ctx": ctx_to},
            device_id_type=MESH,
        )

    def piece_arrived(which, plane, slot, from_core):
        place = bufs[which].at[plane * 4 + slot, token_rows(from_core)]
        pltpu.make_async_remote_copy(
            src_ref=place,
            dst_ref=place,
            send_sem=send_sems.at[0, 0],
            recv_sem=recv_sems.at[plane, slot, which, from_core],
            device_id={"head": z, "ctx": sib},
            device_id_type=MESH,
        ).wait_recv()

    def whole_arrived(which, k, slot):
        whole(which, k, slot, 0, z, sib).wait_recv()

    def swap(src, dst, number):
        return pltpu.make_async_remote_copy(
            src_ref=src,
            dst_ref=dst,
            send_sem=swap_send.at[number],
            recv_sem=swap_recv.at[number],
            device_id={"head": z, "ctx": sib},
            device_id_type=MESH,
        )

    q_swap = swap(q_ref.at[:, columns(other, heads * HD)], q_in.at[core], 0)
    q_got = swap(q_in.at[other], q_in.at[other], 0)

    def own_pieces():
        for which in (0, 1):
            for cross, to_core in enumerate((core, other)):
                number = 2 * which + cross

                @pl.when(z < planes - 1)
                def _():
                    piece(which, to_core, number, z + 1, 2 * chip + to_core).start()

                piece(which, to_core, 4 + number, z, 2 * x_chip + to_core).start()
                piece(which, to_core, 8 + number, z, 2 * y_chip + to_core).start()
            piece(which, other, 12 + which, z, sib).start()

    def column(k):
        @pl.when(z >= k)
        def _():
            for which in (0, 1):
                if k == 1:
                    piece_arrived(which, z - 1, chip, core)
                    piece_arrived(which, z - 1, chip, other)
                else:
                    whole_arrived(which, k, chip)

                @pl.when(z < planes - 1)
                def _():
                    whole(which, k, chip, which, z + 1, ctx).start()

                whole(which, k, chip, 2 + which, z, 2 * x_chip + core).start()
                whole(which, k, chip, 4 + which, z, 2 * y_chip + core).start()

    def side_arrived(which, k, slot):
        if k == 0:
            piece_arrived(which, z, slot, core)
            piece_arrived(which, z, slot, other)
        else:
            whole_arrived(which, k, slot)

    def across(k):
        @pl.when(z >= k)
        def _():
            side_arrived(0, k, x_chip)
            whole(0, k, x_chip, 14, z, 2 * y_chip + core).start()
            side_arrived(1, k, y_chip)
            whole(1, k, y_chip, 15, z, 2 * x_chip + core).start()

    def rest(k):
        @pl.when(z >= k)
        def _():
            side_arrived(1, k, x_chip)
            side_arrived(0, k, y_chip)
            if k == 0:
                for which in (0, 1):
                    piece_arrived(which, z, chip, other)
            for which in (0, 1):
                whole_arrived(which, k, d_chip)

    def sent(k):
        @pl.when(z >= k)
        def _():
            if k == 0:
                @pl.when(z < planes - 1)
                def _():
                    for kind in range(4):
                        piece(0, core, kind, z, sib).wait_send()

                for kind in range(4, 14):
                    piece(0, core, kind, z, sib).wait_send()
            else:
                @pl.when(z < planes - 1)
                def _():
                    for kind in range(2):
                        whole(0, k, chip, kind, z, sib).wait_send()

                for kind in range(2, 6):
                    whole(0, k, chip, kind, z, sib).wait_send()
            for kind in (14, 15):
                whole(0, k, chip, kind, z, sib).wait_send()

    def prepare():
        for copy in local_copies:
            copy.wait()
        listed = lists[...]
        width = listed.shape[0]
        spot = lax.broadcasted_iota(jnp.int32, listed.shape, 0)
        last = jnp.min(jnp.where(listed == query_block, spot, width), axis=0, keepdims=True)
        listed = jnp.where(spot <= last, listed, -1)
        block = lax.broadcasted_iota(jnp.int32, (HD, H), 0)
        bias = jnp.full((HD, H), MASKED, jnp.float32)
        for e in range(width):
            bias = jnp.where(listed[e:e + 1, :] == block, 0.0, bias)
        bias_by_block[...] = jnp.zeros_like(bias_by_block)
        bias_by_block[:, :H] = bias
        bias_by_head[...] = bias_by_block[...].T
        q_got.wait_recv()
        for h in range(heads):
            group, row = h // per_group, (h % per_group) * both
            for part in (0, 1):
                start = row + part * tokens
                q_ext[group, start:start + tokens, :HD] = q_in[part, :, h * HD:(h + 1) * HD]
            q_ext[group, row:row + both, HD:] = jnp.broadcast_to(
                bias_by_head[pl.ds(core * heads + h, 1), :], (both, HD)
            ).astype(jnp.bfloat16)

    keys_here = 4 * both
    cuts = [slice(i * HD, (i + 1) * HD) for i in range(keys_here // HD)]
    factor = LOG2E / math.sqrt(HD)

    def attend(k, group):
        @pl.when(z >= k)
        def _():
            plane = z - k
            key_row = lax.broadcasted_iota(jnp.int32, (keys_here, HD), 0)
            key_lane = lax.broadcasted_iota(jnp.int32, (keys_here, HD), 1)
            block_of = (plane * keys_here + key_row) // BLOCK
            onehot = jnp.where(block_of == key_lane, 1.0, 0.0).astype(jnp.bfloat16)
            cols = slice(group * HD, (group + 1) * HD)
            key = k_all[pl.ds(plane * 4, 4), :, cols].reshape(keys_here, HD)
            value = v_all[pl.ds(plane * 4, 4), :, cols].reshape(keys_here, HD)
            s = lax.dot_general(
                q_ext[group],
                jnp.concatenate([key, onehot], axis=1),
                (((1,), (1,)), ((), ())),
                preferred_element_type=jnp.float32,
            )
            if k == 0:
                row_pos = chip * both + lax.broadcasted_iota(jnp.int32, s.shape, 0) % both
                col_pos = lax.broadcasted_iota(jnp.int32, s.shape, 1)
                s = jnp.where(col_pos <= row_pos, s, MASKED)
            high = s[:, cuts[0]]
            for cut in cuts[1:]:
                high = jnp.maximum(high, s[:, cut])
            high = jnp.broadcast_to(jnp.max(high, axis=1, keepdims=True), (rows, HD))
            if k > 0:
                old = top[group]
                high = jnp.maximum(high, old)
                shrink = jnp.exp2((old - high) * factor)
            parts = [jnp.exp2((s[:, cut] - high) * factor) for cut in cuts]
            w = jnp.concatenate([part.astype(jnp.bfloat16) for part in parts], axis=1)
            part = parts[0]
            for more in parts[1:]:
                part = part + more
            mixed = jnp.dot(w, value, preferred_element_type=jnp.float32)
            if k > 0:
                part = part + total[group] * shrink
                mixed = mixed + acc[group] * shrink
            top[group] = high
            total[group] = part
            acc[group] = mixed

    own_pieces()
    q_swap.start()
    prepare()
    across(0)
    column(1)
    rest(0)
    for k in range(4):
        attend(k, 0)
        if k < 3:
            across(k + 1)
        if k < 2:
            column(k + 2)
        attend(k, 1)
        if k < 3:
            rest(k + 1)

    mine = pl.ds(core * heads, heads)
    home = swap(leaving, done.at[mine], 1)
    for group in range(groups):
        summed = jnp.sum(total[group], axis=1, keepdims=True)
        result = (acc[group] / summed).astype(jnp.bfloat16)
        result = result.reshape(per_group, 2, tokens, HD)
        here = jnp.where(core == 0, result[:, 0], result[:, 1])
        there = jnp.where(core == 0, result[:, 1], result[:, 0])
        done[pl.ds(core * heads + group * per_group, per_group)] = here
        leaving[group * per_group:(group + 1) * per_group] = there
    home.start()
    for k in range(4):
        sent(k)
    q_swap.wait_send()
    swap(leaving, done.at[pl.ds(other * heads, heads)], 1).wait_recv()
    for place in range(H):
        out_ref[:, place * HD:(place + 1) * HD] = done[order_ref[place]]
    home.wait_send()


def planes_local(queries, keys, values, block_index, block_count, head_order):
    tokens = queries.shape[0]
    planes = lax.axis_size("head")
    rows = H // KVH * 2 * tokens
    groups = KVH // 2
    table = block_index.transpose(0, 2, 1)
    any_spec = pl.BlockSpec(memory_space=pl.ANY)
    return pl.pallas_call(
        plane_kernel,
        out_shape=jax.ShapeDtypeStruct(queries.shape, jnp.bfloat16),
        in_specs=[any_spec] * 4 + [pl.BlockSpec(memory_space=pltpu.SMEM)],
        out_specs=pl.BlockSpec(memory_space=pltpu.VMEM),
        scratch_shapes=[
            pltpu.VMEM((planes * 4, 2 * tokens, groups * HD), jnp.bfloat16),
            pltpu.VMEM((planes * 4, 2 * tokens, groups * HD), jnp.bfloat16),
            pltpu.VMEM((2, tokens, H // 2 * HD), jnp.bfloat16),
            pltpu.VMEM((groups, rows, 2 * HD), jnp.bfloat16),
            pltpu.VMEM((groups, rows, HD), jnp.float32),
            pltpu.VMEM((groups, rows, HD), jnp.float32),
            pltpu.VMEM((groups, rows, HD), jnp.float32),
            pltpu.VMEM(table.shape[1:], jnp.int32),
            pltpu.VMEM((HD, HD), jnp.float32),
            pltpu.VMEM((HD, HD), jnp.float32),
            pltpu.VMEM((H, tokens, HD), jnp.bfloat16),
            pltpu.VMEM((H // 2, tokens, HD), jnp.bfloat16),
            pltpu.SemaphoreType.DMA((4,)),
            pltpu.SemaphoreType.DMA((2,)),
            pltpu.SemaphoreType.DMA((2,)),
            pltpu.SemaphoreType.DMA((planes, 16)),
            pltpu.SemaphoreType.DMA((planes, 4, 2, 2)),
        ],
        compiler_params=pltpu.CompilerParams(
            collective_id=0, has_side_effects=True, vmem_limit_bytes=60 * 1024 * 1024
        ),
    )(queries, keys, values, table, head_order)


def solution(mesh):
    in_planes = mesh.shape["head"] == 4 and mesh.shape["ctx"] == 8
    return jax.shard_map(
        planes_local if in_planes else local,
        mesh=mesh,
        in_specs=(
            P(("head", "ctx"), None),
            P(("head", "ctx"), None),
            P(("head", "ctx"), None),
            P(),
            P(),
            P(),
        ),
        out_specs=P(("head", "ctx"), None),
        check_vma=False,
    )
```

```python
from functools import partial
import math

import jax
import jax.numpy as jnp
from jax import lax
from jax.experimental import pallas as pl
from jax.experimental.pallas import tpu as pltpu
from jax.sharding import PartitionSpec as P

H = 28
KVH = 4
HD = 128
BLOCK = 128


FLOOR = -1e30
MESH = pl.DeviceIdType.MESH


def positions(stripes, stripe_len, device, ctx_total):
    offsets = jnp.arange(stripes * stripe_len, dtype=jnp.int32)
    stripe = offsets // stripe_len
    return (stripe * ctx_total + device) * stripe_len + offsets % stripe_len


def keep_state(carried):
    return carried


def update_lanes(query_rows, key_lanes, value_lanes, allowed, score_scale, carried):
    running_max, running_sum, running_out = carried
    scores = (
        jnp.einsum("qgd,kgd->qgk", query_rows, key_lanes, preferred_element_type=jnp.float32)
        * score_scale
    )
    scores = jnp.where(allowed, scores, FLOOR)
    new_max = jnp.maximum(running_max, jnp.max(scores, axis=2))
    weights = jnp.where(allowed, jnp.exp(scores - new_max[:, :, None]), 0.0)
    factor = jnp.exp(running_max - new_max)
    new_sum = running_sum * factor + jnp.sum(weights, axis=2)
    update = jnp.einsum(
        "qgk,kgd->qgd",
        weights.astype(jnp.bfloat16),
        value_lanes,
        preferred_element_type=jnp.float32,
    )
    new_out = running_out * factor[:, :, None] + update
    return (new_max, new_sum, new_out)


def local(queries, keys, values, block_index, block_count, head_order):
    local_tokens = queries.shape[0]
    per_group = H // KVH
    head_total = lax.axis_size("head")
    ctx_total = lax.axis_size("ctx")
    ctx_here = lax.axis_index("ctx")
    head_here = lax.axis_index("head")
    query_split = queries.reshape(local_tokens, H, HD)
    key_split = keys.reshape(local_tokens, KVH, HD)
    value_split = values.reshape(local_tokens, KVH, HD)
    query_sorted = jnp.take(query_split, head_order, axis=1)
    kv_lists = (head_order // per_group).reshape(head_total, per_group)
    kv_pairs = jnp.stack([jnp.min(kv_lists, axis=1), jnp.max(kv_lists, axis=1)], axis=1).reshape(
        head_total * 2
    )
    key_sent = jnp.take(key_split, kv_pairs, axis=1).reshape(local_tokens, head_total, 2, HD)
    value_sent = jnp.take(value_split, kv_pairs, axis=1).reshape(local_tokens, head_total, 2, HD)
    own_heads = lax.dynamic_slice_in_dim(head_order, head_here * per_group, per_group)
    own_kv = own_heads // per_group
    slot_of = (own_kv == jnp.max(own_kv)).astype(jnp.int32)
    query_sent = query_sorted.reshape(local_tokens, head_total, per_group, HD)
    query_got, key_got, value_got = (
        lax.all_to_all(query_sent, "head", split_axis=1, concat_axis=0, tiled=True),
        lax.all_to_all(key_sent, "head", split_axis=1, concat_axis=0, tiled=True),
        lax.all_to_all(value_sent, "head", split_axis=1, concat_axis=0, tiled=True),
    )
    row_count = head_total * local_tokens
    slot_count = key_sent.shape[2]
    query_rows = query_got.reshape(row_count, per_group, HD)
    key_rows = key_got.reshape(row_count, slot_count, HD)
    value_rows = value_got.reshape(row_count, slot_count, HD)
    query_pos = positions(head_total, local_tokens, ctx_here, ctx_total)
    per_entry = min(local_tokens, BLOCK)
    entries = row_count // per_entry
    entry_blocks = query_pos[::per_entry] // BLOCK
    block_total = block_index.shape[2]
    block_iota = jnp.arange(block_total, dtype=jnp.int32)
    listed = jnp.take(jnp.take(block_index, entry_blocks, axis=0), own_heads, axis=1)
    counted = jnp.take(jnp.take(block_count, entry_blocks, axis=0), own_heads, axis=1)
    usable = block_iota[None, None, :] < counted[:, :, None]
    block_hits = (listed[:, :, :, None] == block_iota[None, None, None, :]) & usable[:, :, :, None]
    table_flags = jnp.any(block_hits, axis=2).astype(jnp.bfloat16)
    score_scale = 1.0 / math.sqrt(HD)
    initial = (
        jnp.full((row_count, per_group), FLOOR, jnp.float32),
        jnp.zeros((row_count, per_group), jnp.float32),
        jnp.zeros((row_count, per_group, HD), jnp.float32),
    )
    key_piece = lax.all_gather(key_rows, "ctx", axis=0, tiled=True)
    value_piece = lax.all_gather(value_rows, "ctx", axis=0, tiled=True)
    shard_total = key_piece.shape[0] // row_count

    def one_shard(number, inner_state):
        key_block = lax.dynamic_slice_in_dim(key_piece, number * row_count, row_count, 0)
        value_block = lax.dynamic_slice_in_dim(value_piece, number * row_count, row_count, 0)
        key_lanes = jnp.take(key_block, slot_of, axis=1)
        value_lanes = jnp.take(value_block, slot_of, axis=1)
        key_pos = positions(head_total, local_tokens, number, ctx_total)
        onehot = (block_iota[:, None] == (key_pos // BLOCK)[None, :]).astype(jnp.bfloat16)
        chosen = jnp.einsum("egb,bk->egk", table_flags, onehot, preferred_element_type=jnp.float32)
        spread = jnp.broadcast_to(
            chosen[:, None], (entries, per_entry, per_group, row_count)
        ).reshape(row_count, per_group, row_count)
        allowed = (spread > 0.5) & (key_pos[None, None, :] <= query_pos[:, None, None])
        return lax.cond(
            jnp.any(allowed),
            partial(update_lanes, query_rows, key_lanes, value_lanes, allowed, score_scale),
            keep_state,
            inner_state,
        )

    folded = lax.fori_loop(0, shard_total, one_shard, initial)
    running_max, running_sum, running_out = folded
    attended = (
        (running_out / running_sum[:, :, None])
        .astype(jnp.bfloat16)
        .reshape(row_count, 1, per_group, HD)
    )
    returned = lax.all_to_all(attended, "head", split_axis=0, concat_axis=1, tiled=True).reshape(
        local_tokens, H, HD
    )
    return returned.reshape(local_tokens, H * HD)


MASKED = -1e30


def plane_kernel(
    q_ref, k_ref, v_ref, table_ref, order_ref, out_ref,
    k_all, v_all, q_in, q_rows, q_ext, acc, top, total, lists, bias_by_block, bias_by_head,
    done, leaving, local_sems, swap_send, swap_recv, send_sems, recv_sems,
):
    z = lax.axis_index("head")
    ctx = lax.axis_index("ctx")
    planes = lax.axis_size("head")
    tokens = q_ref.shape[0]
    per_group = H // KVH
    groups = KVH // 2
    heads = H // 2
    both = 2 * tokens
    rows = per_group * both
    half = groups * HD
    core = ctx % 2
    other = 1 - core
    chip = ctx // 2
    x_chip = chip + 1 - 2 * (chip % 2)
    y_chip = chip + 2 - 4 * (chip // 2)
    d_chip = x_chip + y_chip - chip
    sib = 2 * chip + other
    query_block = (z * 4 + chip) * both // BLOCK
    bufs = (k_all, v_all)
    heres = (k_ref, v_ref)

    def columns(which_core, width):
        return pl.ds(pl.multiple_of(which_core * width, width), width)

    def token_rows(which_core):
        return pl.ds(pl.multiple_of(which_core * tokens, tokens), tokens)

    local_copies = [
        pltpu.make_async_copy(
            q_ref.at[:, columns(core, heads * HD)], q_in.at[core], local_sems.at[0]
        ),
        pltpu.make_async_copy(table_ref.at[query_block], lists, local_sems.at[1]),
    ]
    for which in (0, 1):
        local_copies.append(pltpu.make_async_copy(
            heres[which].at[:, columns(core, half)],
            bufs[which].at[z * 4 + chip, token_rows(core)],
            local_sems.at[2 + which],
        ))
    for copy in local_copies:
        copy.start()

    barrier = pltpu.get_barrier_semaphore()

    def greet(head_to, ctx_to):
        pl.semaphore_signal(
            barrier, inc=1, device_id={"head": head_to, "ctx": ctx_to}, device_id_type=MESH
        )

    greet(z, sib)
    for which_core in (core, other):
        greet(z, 2 * x_chip + which_core)
        greet(z, 2 * y_chip + which_core)

    @pl.when(z > 0)
    def _():
        greet(z - 1, ctx)
        greet(z - 1, sib)

    @pl.when(z < planes - 1)
    def _():
        greet(z + 1, ctx)
        greet(z + 1, sib)

    pl.semaphore_wait(
        barrier, 5 + 2 * (z > 0).astype(jnp.int32) + 2 * (z < planes - 1).astype(jnp.int32)
    )

    def piece(which, to_core, kind, head_to, ctx_to):
        return pltpu.make_async_remote_copy(
            src_ref=heres[which].at[:, columns(to_core, half)],
            dst_ref=bufs[which].at[z * 4 + chip, token_rows(core)],
            send_sem=send_sems.at[0, kind],
            recv_sem=recv_sems.at[z, chip, which, core],
            device_id={"head": head_to, "ctx": ctx_to},
            device_id_type=MESH,
        )

    def whole(which, k, slot, kind, head_to, ctx_to):
        place = bufs[which].at[(z - k) * 4 + slot]
        return pltpu.make_async_remote_copy(
            src_ref=place,
            dst_ref=place,
            send_sem=send_sems.at[k, kind],
            recv_sem=recv_sems.at[z - k, slot, which, 0],
            device_id={"head": head_to, "ctx": ctx_to},
            device_id_type=MESH,
        )

    def piece_arrived(which, plane, slot, from_core):
        place = bufs[which].at[plane * 4 + slot, token_rows(from_core)]
        pltpu.make_async_remote_copy(
            src_ref=place,
            dst_ref=place,
            send_sem=send_sems.at[0, 0],
            recv_sem=recv_sems.at[plane, slot, which, from_core],
            device_id={"head": z, "ctx": sib},
            device_id_type=MESH,
        ).wait_recv()

    def whole_arrived(which, k, slot):
        whole(which, k, slot, 0, z, sib).wait_recv()

    def swap(src, dst, number):
        return pltpu.make_async_remote_copy(
            src_ref=src,
            dst_ref=dst,
            send_sem=swap_send.at[number],
            recv_sem=swap_recv.at[number],
            device_id={"head": z, "ctx": sib},
            device_id_type=MESH,
        )

    q_swap = swap(q_ref.at[:, columns(other, heads * HD)], q_in.at[core], 0)
    q_got = swap(q_in.at[other], q_in.at[other], 0)

    def own_pieces():
        for which in (0, 1):
            for cross, to_core in enumerate((core, other)):
                number = 2 * which + cross

                @pl.when(z < planes - 1)
                def _():
                    piece(which, to_core, number, z + 1, 2 * chip + to_core).start()

                piece(which, to_core, 4 + number, z, 2 * x_chip + to_core).start()
                piece(which, to_core, 8 + number, z, 2 * y_chip + to_core).start()
            piece(which, other, 12 + which, z, sib).start()

    def column(k):
        @pl.when(z >= k)
        def _():
            for which in (0, 1):
                if k == 1:
                    piece_arrived(which, z - 1, chip, core)
                    piece_arrived(which, z - 1, chip, other)
                else:
                    whole_arrived(which, k, chip)

                @pl.when(z < planes - 1)
                def _():
                    whole(which, k, chip, which, z + 1, ctx).start()

                whole(which, k, chip, 2 + which, z, 2 * x_chip + core).start()
                whole(which, k, chip, 4 + which, z, 2 * y_chip + core).start()

    def side_arrived(which, k, slot):
        if k == 0:
            piece_arrived(which, z, slot, core)
            piece_arrived(which, z, slot, other)
        else:
            whole_arrived(which, k, slot)

    def across(k):
        @pl.when(z >= k)
        def _():
            side_arrived(0, k, x_chip)
            whole(0, k, x_chip, 14, z, 2 * y_chip + core).start()
            side_arrived(1, k, y_chip)
            whole(1, k, y_chip, 15, z, 2 * x_chip + core).start()

    def rest(k):
        @pl.when(z >= k)
        def _():
            side_arrived(1, k, x_chip)
            side_arrived(0, k, y_chip)
            if k == 0:
                for which in (0, 1):
                    piece_arrived(which, z, chip, other)
            for which in (0, 1):
                whole_arrived(which, k, d_chip)

    def sent(k):
        @pl.when(z >= k)
        def _():
            if k == 0:
                @pl.when(z < planes - 1)
                def _():
                    for kind in range(4):
                        piece(0, core, kind, z, sib).wait_send()

                for kind in range(4, 14):
                    piece(0, core, kind, z, sib).wait_send()
            else:
                @pl.when(z < planes - 1)
                def _():
                    for kind in range(2):
                        whole(0, k, chip, kind, z, sib).wait_send()

                for kind in range(2, 6):
                    whole(0, k, chip, kind, z, sib).wait_send()
            for kind in (14, 15):
                whole(0, k, chip, kind, z, sib).wait_send()

    def prepare():
        for copy in local_copies:
            copy.wait()
        listed = lists[...]
        width = listed.shape[0]
        spot = lax.broadcasted_iota(jnp.int32, listed.shape, 0)
        last = jnp.min(jnp.where(listed == query_block, spot, width), axis=0, keepdims=True)
        listed = jnp.where(spot <= last, listed, -1)
        block = lax.broadcasted_iota(jnp.int32, (HD, H), 0)
        bias = jnp.full((HD, H), MASKED, jnp.float32)
        for e in range(width):
            bias = jnp.where(listed[e:e + 1, :] == block, 0.0, bias)
        bias_by_block[...] = jnp.zeros_like(bias_by_block)
        bias_by_block[:, :H] = bias
        bias_by_head[...] = bias_by_block[...].T
        q_got.wait_recv()
        for h in range(heads):
            group, row = h // per_group, (h % per_group) * both
            for part in (0, 1):
                start = row + part * tokens
                q_rows[group, start:start + tokens, :HD] = q_in[part, :, h * HD:(h + 1) * HD]
            q_rows[group, row:row + both, HD:] = jnp.broadcast_to(
                bias_by_head[pl.ds(core * heads + h, 1), :], (both, HD)
            ).astype(jnp.bfloat16)
        for group in range(groups):
            q_ext[group] = q_rows[group].T

    keys_here = 4 * both
    scale = 1.0 / math.sqrt(HD)
    chunks = [slice(i, min(i + 2 * HD, rows)) for i in range(0, rows, 2 * HD)]

    def attend(k, group):
        @pl.when(z >= k)
        def _():
            plane = z - k
            key_row = lax.broadcasted_iota(jnp.int32, (keys_here, HD), 0)
            key_lane = lax.broadcasted_iota(jnp.int32, (keys_here, HD), 1)
            block_of = (plane * keys_here + key_row) // BLOCK
            onehot = jnp.where(block_of == key_lane, 1.0, 0.0).astype(jnp.bfloat16)
            cols = slice(group * HD, (group + 1) * HD)
            key = k_all[pl.ds(plane * 4, 4), :, cols].reshape(keys_here, HD)
            value = v_all[pl.ds(plane * 4, 4), :, cols].reshape(keys_here, HD).T
            key = jnp.concatenate([key, onehot], axis=1)
            for chunk in chunks:
                s = jnp.dot(key, q_ext[group, :, chunk], preferred_element_type=jnp.float32)
                if k == 0:
                    row_pos = chip * both + lax.broadcasted_iota(jnp.int32, s.shape, 1) % both
                    key_pos = lax.broadcasted_iota(jnp.int32, s.shape, 0)
                    s = jnp.where(key_pos <= row_pos, s, MASKED)
                high = jnp.max(s, axis=0, keepdims=True)
                if k > 0:
                    old = top[group, :, chunk]
                    high = jnp.maximum(high, old)
                    shrink = jnp.exp((old - high) * scale)
                w = jnp.exp((s - high) * scale)
                part = jnp.sum(w, axis=0, keepdims=True)
                mixed = jnp.dot(value, w.astype(jnp.bfloat16), preferred_element_type=jnp.float32)
                if k > 0:
                    part = part + total[group, :, chunk] * shrink
                    mixed = mixed + acc[group, :, chunk] * shrink
                top[group, :, chunk] = high
                total[group, :, chunk] = part
                acc[group, :, chunk] = mixed

    own_pieces()
    q_swap.start()
    prepare()
    across(0)
    column(1)
    rest(0)
    for k in range(4):
        attend(k, 0)
        if k < 3:
            across(k + 1)
        if k < 2:
            column(k + 2)
        attend(k, 1)
        if k < 3:
            rest(k + 1)

    mine = pl.ds(core * heads, heads)
    home = swap(leaving, done.at[mine], 1)
    for group in range(groups):
        result = (acc[group] / total[group]).T.astype(jnp.bfloat16)
        result = result.reshape(per_group, 2, tokens, HD)
        here = jnp.where(core == 0, result[:, 0], result[:, 1])
        there = jnp.where(core == 0, result[:, 1], result[:, 0])
        done[pl.ds(core * heads + group * per_group, per_group)] = here
        leaving[group * per_group:(group + 1) * per_group] = there
    home.start()
    for k in range(4):
        sent(k)
    q_swap.wait_send()
    swap(leaving, done.at[pl.ds(other * heads, heads)], 1).wait_recv()
    for place in range(H):
        out_ref[:, place * HD:(place + 1) * HD] = done[order_ref[place]]
    home.wait_send()


def planes_local(queries, keys, values, block_index, block_count, head_order):
    tokens = queries.shape[0]
    planes = lax.axis_size("head")
    rows = H // KVH * 2 * tokens
    groups = KVH // 2
    table = block_index.transpose(0, 2, 1)
    hbm_spec = pl.BlockSpec(memory_space=pltpu.HBM)
    return pl.pallas_call(
        plane_kernel,
        out_shape=jax.ShapeDtypeStruct(queries.shape, jnp.bfloat16),
        in_specs=[hbm_spec] * 4 + [pl.BlockSpec(memory_space=pltpu.SMEM)],
        out_specs=pl.BlockSpec(memory_space=pltpu.VMEM),
        scratch_shapes=[
            pltpu.VMEM((planes * 4, 2 * tokens, groups * HD), jnp.bfloat16),
            pltpu.VMEM((planes * 4, 2 * tokens, groups * HD), jnp.bfloat16),
            pltpu.VMEM((2, tokens, H // 2 * HD), jnp.bfloat16),
            pltpu.VMEM((groups, rows, 2 * HD), jnp.bfloat16),
            pltpu.VMEM((groups, 2 * HD, rows), jnp.bfloat16),
            pltpu.VMEM((groups, HD, rows), jnp.float32),
            pltpu.VMEM((groups, 1, rows), jnp.float32),
            pltpu.VMEM((groups, 1, rows), jnp.float32),
            pltpu.VMEM(table.shape[1:], jnp.int32),
            pltpu.VMEM((HD, HD), jnp.float32),
            pltpu.VMEM((HD, HD), jnp.float32),
            pltpu.VMEM((H, tokens, HD), jnp.bfloat16),
            pltpu.VMEM((H // 2, tokens, HD), jnp.bfloat16),
            pltpu.SemaphoreType.DMA((4,)),
            pltpu.SemaphoreType.DMA((2,)),
            pltpu.SemaphoreType.DMA((2,)),
            pltpu.SemaphoreType.DMA((planes, 16)),
            pltpu.SemaphoreType.DMA((planes, 4, 2, 2)),
        ],
        compiler_params=pltpu.CompilerParams(
            collective_id=0, has_side_effects=True, vmem_limit_bytes=40 * 1024 * 1024
        ),
    )(queries, keys, values, table, head_order)


def solution(mesh):
    in_planes = mesh.shape["head"] == 4 and mesh.shape["ctx"] == 8
    return jax.shard_map(
        planes_local if in_planes else local,
        mesh=mesh,
        in_specs=(
            P(("head", "ctx"), None),
            P(("head", "ctx"), None),
            P(("head", "ctx"), None),
            P(),
            P(),
            P(),
        ),
        out_specs=P(("head", "ctx"), None),
        check_vma=False,
    )
```

```python
from functools import partial
import math

import jax
import jax.numpy as jnp
from jax import lax
from jax.experimental import pallas as pl
from jax.experimental.pallas import tpu as pltpu
from jax.sharding import PartitionSpec as P

H = 28
KVH = 4
HD = 128
BLOCK = 128


FLOOR = -1e30
MESH = pl.DeviceIdType.MESH


def positions(stripes, stripe_len, device, ctx_total):
    offsets = jnp.arange(stripes * stripe_len, dtype=jnp.int32)
    stripe = offsets // stripe_len
    return (stripe * ctx_total + device) * stripe_len + offsets % stripe_len


def keep_state(carried):
    return carried


def update_lanes(query_rows, key_lanes, value_lanes, allowed, score_scale, carried):
    running_max, running_sum, running_out = carried
    scores = (
        jnp.einsum("qgd,kgd->qgk", query_rows, key_lanes, preferred_element_type=jnp.float32)
        * score_scale
    )
    scores = jnp.where(allowed, scores, FLOOR)
    new_max = jnp.maximum(running_max, jnp.max(scores, axis=2))
    weights = jnp.where(allowed, jnp.exp(scores - new_max[:, :, None]), 0.0)
    factor = jnp.exp(running_max - new_max)
    new_sum = running_sum * factor + jnp.sum(weights, axis=2)
    update = jnp.einsum(
        "qgk,kgd->qgd",
        weights.astype(jnp.bfloat16),
        value_lanes,
        preferred_element_type=jnp.float32,
    )
    new_out = running_out * factor[:, :, None] + update
    return (new_max, new_sum, new_out)


def local(queries, keys, values, block_index, block_count, head_order):
    local_tokens = queries.shape[0]
    per_group = H // KVH
    head_total = lax.axis_size("head")
    ctx_total = lax.axis_size("ctx")
    ctx_here = lax.axis_index("ctx")
    head_here = lax.axis_index("head")
    query_split = queries.reshape(local_tokens, H, HD)
    key_split = keys.reshape(local_tokens, KVH, HD)
    value_split = values.reshape(local_tokens, KVH, HD)
    query_sorted = jnp.take(query_split, head_order, axis=1)
    kv_lists = (head_order // per_group).reshape(head_total, per_group)
    kv_pairs = jnp.stack([jnp.min(kv_lists, axis=1), jnp.max(kv_lists, axis=1)], axis=1).reshape(
        head_total * 2
    )
    key_sent = jnp.take(key_split, kv_pairs, axis=1).reshape(local_tokens, head_total, 2, HD)
    value_sent = jnp.take(value_split, kv_pairs, axis=1).reshape(local_tokens, head_total, 2, HD)
    own_heads = lax.dynamic_slice_in_dim(head_order, head_here * per_group, per_group)
    own_kv = own_heads // per_group
    slot_of = (own_kv == jnp.max(own_kv)).astype(jnp.int32)
    query_sent = query_sorted.reshape(local_tokens, head_total, per_group, HD)
    query_got, key_got, value_got = (
        lax.all_to_all(query_sent, "head", split_axis=1, concat_axis=0, tiled=True),
        lax.all_to_all(key_sent, "head", split_axis=1, concat_axis=0, tiled=True),
        lax.all_to_all(value_sent, "head", split_axis=1, concat_axis=0, tiled=True),
    )
    row_count = head_total * local_tokens
    slot_count = key_sent.shape[2]
    query_rows = query_got.reshape(row_count, per_group, HD)
    key_rows = key_got.reshape(row_count, slot_count, HD)
    value_rows = value_got.reshape(row_count, slot_count, HD)
    query_pos = positions(head_total, local_tokens, ctx_here, ctx_total)
    per_entry = min(local_tokens, BLOCK)
    entries = row_count // per_entry
    entry_blocks = query_pos[::per_entry] // BLOCK
    block_total = block_index.shape[2]
    block_iota = jnp.arange(block_total, dtype=jnp.int32)
    listed = jnp.take(jnp.take(block_index, entry_blocks, axis=0), own_heads, axis=1)
    counted = jnp.take(jnp.take(block_count, entry_blocks, axis=0), own_heads, axis=1)
    usable = block_iota[None, None, :] < counted[:, :, None]
    block_hits = (listed[:, :, :, None] == block_iota[None, None, None, :]) & usable[:, :, :, None]
    table_flags = jnp.any(block_hits, axis=2).astype(jnp.bfloat16)
    score_scale = 1.0 / math.sqrt(HD)
    initial = (
        jnp.full((row_count, per_group), FLOOR, jnp.float32),
        jnp.zeros((row_count, per_group), jnp.float32),
        jnp.zeros((row_count, per_group, HD), jnp.float32),
    )
    key_piece = lax.all_gather(key_rows, "ctx", axis=0, tiled=True)
    value_piece = lax.all_gather(value_rows, "ctx", axis=0, tiled=True)
    shard_total = key_piece.shape[0] // row_count

    def one_shard(number, inner_state):
        key_block = lax.dynamic_slice_in_dim(key_piece, number * row_count, row_count, 0)
        value_block = lax.dynamic_slice_in_dim(value_piece, number * row_count, row_count, 0)
        key_lanes = jnp.take(key_block, slot_of, axis=1)
        value_lanes = jnp.take(value_block, slot_of, axis=1)
        key_pos = positions(head_total, local_tokens, number, ctx_total)
        onehot = (block_iota[:, None] == (key_pos // BLOCK)[None, :]).astype(jnp.bfloat16)
        chosen = jnp.einsum("egb,bk->egk", table_flags, onehot, preferred_element_type=jnp.float32)
        spread = jnp.broadcast_to(
            chosen[:, None], (entries, per_entry, per_group, row_count)
        ).reshape(row_count, per_group, row_count)
        allowed = (spread > 0.5) & (key_pos[None, None, :] <= query_pos[:, None, None])
        return lax.cond(
            jnp.any(allowed),
            partial(update_lanes, query_rows, key_lanes, value_lanes, allowed, score_scale),
            keep_state,
            inner_state,
        )

    folded = lax.fori_loop(0, shard_total, one_shard, initial)
    running_max, running_sum, running_out = folded
    attended = (
        (running_out / running_sum[:, :, None])
        .astype(jnp.bfloat16)
        .reshape(row_count, 1, per_group, HD)
    )
    returned = lax.all_to_all(attended, "head", split_axis=0, concat_axis=1, tiled=True).reshape(
        local_tokens, H, HD
    )
    return returned.reshape(local_tokens, H * HD)


MASKED = -1e30


def plane_kernel(
    q_ref, k_ref, v_ref, table_ref, order_ref, out_ref,
    k_all, v_all, q_in, q_rows, q_ext, acc, top, total, lists, bias_by_block,
    bias_by_head, done, leaving, local_sems, piece_send, piece_recv, head_send, head_recv,
    send_sems, recv_sems,
):
    z = lax.axis_index("head")
    ctx = lax.axis_index("ctx")
    planes = lax.axis_size("head")
    tokens = q_ref.shape[0]
    per_group = H // KVH
    width = per_group * HD
    rows = 4 * per_group * tokens
    lane_keys = 4 * tokens
    core = ctx % 2
    other = 1 - core
    chip = ctx // 2
    x_chip = chip + 1 - 2 * (chip % 2)
    y_chip = chip + 2 - 4 * (chip // 2)
    d_chip = x_chip + y_chip - chip
    away = (d_chip, x_chip, y_chip)
    sib = 2 * chip + other
    bufs = (k_all, v_all)
    heres = (k_ref, v_ref)

    def head_columns(of_chip, size):
        return pl.ds(pl.multiple_of(of_chip * size, size), size)

    def chip_rows(of_chip):
        return pl.ds(pl.multiple_of(of_chip * tokens, tokens), tokens)

    own_places = [bufs[which].at[z * 2 + core, chip_rows(chip)] for which in (0, 1)]
    local_copies = [
        pltpu.make_async_copy(
            heres[which].at[:, head_columns(chip, HD)], own_places[which], local_sems.at[which]
        )
        for which in (0, 1)
    ]
    local_copies.append(pltpu.make_async_copy(
        q_ref.at[:, head_columns(chip, width)], q_in.at[3], local_sems.at[2]
    ))
    local_copies.append(pltpu.make_async_copy(
        table_ref.at[pl.ds(z * 4, 4)], lists, local_sems.at[3]
    ))
    for copy in local_copies:
        copy.start()

    barrier = pltpu.get_barrier_semaphore()

    def greet(head_to, ctx_to):
        pl.semaphore_signal(
            barrier, inc=1, device_id={"head": head_to, "ctx": ctx_to}, device_id_type=MESH
        )

    greet(z, sib)
    for near in away:
        greet(z, 2 * near + core)

    @pl.when(z > 0)
    def _():
        greet(z - 1, ctx)

    @pl.when(z < planes - 1)
    def _():
        greet(z + 1, ctx)

    pl.semaphore_wait(
        barrier, 4 + (z > 0).astype(jnp.int32) + (z < planes - 1).astype(jnp.int32)
    )

    def remote(src, dst, send_sem, recv_sem, head_to, ctx_to):
        return pltpu.make_async_remote_copy(
            src_ref=src,
            dst_ref=dst,
            send_sem=send_sem,
            recv_sem=recv_sem,
            device_id={"head": head_to, "ctx": ctx_to},
            device_id_type=MESH,
        )

    def piece(which, r):
        return remote(
            heres[which].at[:, head_columns(away[r], HD)],
            own_places[which],
            piece_send.at[which, r],
            piece_recv.at[which, r],
            z, 2 * away[r] + core,
        )

    def piece_arrived(which, r):
        place = bufs[which].at[z * 2 + core, chip_rows(away[r])]
        remote(
            place, place, piece_send.at[which, r], piece_recv.at[which, r], z, sib
        ).wait_recv()

    def queries_out(r):
        return remote(
            q_ref.at[:, head_columns(away[r], width)],
            q_in.at[r],
            head_send.at[0, r],
            head_recv.at[0, r],
            z, 2 * away[r] + core,
        )

    def result_home(r):
        return remote(
            leaving.at[r],
            done.at[pl.ds(chip * per_group, per_group)],
            head_send.at[1, r],
            head_recv.at[1, r],
            z, 2 * away[r] + core,
        )

    def result_arrived(r):
        remote(
            leaving.at[r],
            done.at[pl.ds(away[r] * per_group, per_group)],
            head_send.at[1, r],
            head_recv.at[1, r],
            z, sib,
        ).wait_recv()

    def whole(which, k, lane, kind, head_to, ctx_to):
        place = bufs[which].at[(z - k) * 2 + lane]
        return remote(
            place, place, send_sems.at[k, kind], recv_sems.at[z - k, lane, which],
            head_to, ctx_to,
        )

    def column(k):
        @pl.when(z >= k)
        def _():
            for which in (0, 1):
                if k == 0:
                    local_copies[which].wait()
                    for r in range(3):
                        piece_arrived(which, r)
                else:
                    whole(which, k, core, 0, z, sib).wait_recv()

                @pl.when(z < planes - 1)
                def _():
                    whole(which, k, core, which, z + 1, ctx).start()

                whole(which, k, core, 2 + which, z, sib).start()

    def beside(k):
        @pl.when(z >= k)
        def _():
            for which in (0, 1):
                whole(which, k, other, 0, z, sib).wait_recv()

    def sent(k):
        @pl.when(z >= k)
        def _():
            @pl.when(z < planes - 1)
            def _():
                for kind in (0, 1):
                    whole(0, k, core, kind, z, sib).wait_send()

            for kind in (2, 3):
                whole(0, k, core, kind, z, sib).wait_send()

    def prepare_bias():
        local_copies[3].wait()
        listed = lists[...]
        entries = listed.shape[1]
        spot = lax.broadcasted_iota(jnp.int32, listed.shape, 1)
        query_block = z * 4 + lax.broadcasted_iota(jnp.int32, listed.shape, 0)
        last = jnp.min(jnp.where(listed == query_block, spot, entries), axis=1, keepdims=True)
        listed = jnp.where(spot <= last, listed, -1)
        bias_by_block[...] = jnp.zeros_like(bias_by_block)
        for chip_here in range(4):
            block = lax.broadcasted_iota(jnp.int32, (entries, H), 0)
            bias = jnp.full((entries, H), MASKED, jnp.float32)
            for e in range(entries):
                bias = jnp.where(listed[chip_here, e:e + 1, :] == block, 0.0, bias)
            bias_by_block[:entries, :H] = bias
            bias_by_head[chip_here] = bias_by_block[...].T

    def prepare_rows(r, of_chip):
        for g in range(per_group):
            row = (r * per_group + g) * tokens
            q_rows[row:row + tokens, :HD] = q_in[r, :, g * HD:(g + 1) * HD]
            q_rows[row:row + tokens, HD:] = jnp.broadcast_to(
                bias_by_head[of_chip, pl.ds(chip * per_group + g, 1), :], (tokens, HD)
            ).astype(jnp.bfloat16)

    keys_here = 2 * lane_keys
    half_rows = rows // 2
    scale = 1.0 / math.sqrt(HD)
    starts = range(0, half_rows, 2 * HD)
    chunks = [
        [slice(h * half_rows + i, h * half_rows + min(i + 2 * HD, half_rows)) for i in starts]
        for h in (0, 1)
    ]

    def attend(k, half):
        @pl.when(z >= k)
        def _():
            plane = z - k
            key_row = lax.broadcasted_iota(jnp.int32, (keys_here, HD), 0)
            key_lane = lax.broadcasted_iota(jnp.int32, (keys_here, HD), 1)
            block_of = plane * 4 + key_row % lane_keys // tokens
            onehot = jnp.where(block_of == key_lane, 1.0, 0.0).astype(jnp.bfloat16)
            key = k_all[pl.ds(plane * 2, 2)].reshape(keys_here, HD)
            value = v_all[pl.ds(plane * 2, 2)].reshape(keys_here, HD).T
            key = jnp.concatenate([key, onehot], axis=1)
            for chunk in chunks[half]:
                s = jnp.dot(key, q_ext[:, chunk], preferred_element_type=jnp.float32)
                if k == 0:
                    key_at = lax.broadcasted_iota(jnp.int32, (keys_here, 1), 0)
                    key_pos = (
                        key_at % lane_keys // tokens * 2 + key_at // lane_keys
                    ) * tokens + key_at % tokens
                    row_at = chunk.start + lax.broadcasted_iota(
                        jnp.int32, (1, chunk.stop - chunk.start), 1
                    )
                    source = row_at // (per_group * tokens)
                    row_chip = jnp.where(
                        source == 0, d_chip,
                        jnp.where(source == 1, x_chip, jnp.where(source == 2, y_chip, chip)),
                    )
                    row_pos = (row_chip * 2 + core) * tokens + row_at % tokens
                    s = jnp.where(key_pos <= row_pos, s, MASKED)
                high = jnp.max(s, axis=0, keepdims=True)
                if k > 0:
                    old = top[:, chunk]
                    high = jnp.maximum(high, old)
                    shrink = jnp.exp((old - high) * scale)
                w = jnp.exp((s - high) * scale)
                part = jnp.sum(w, axis=0, keepdims=True)
                mixed = jnp.dot(value, w.astype(jnp.bfloat16), preferred_element_type=jnp.float32)
                if k > 0:
                    part = part + total[:, chunk] * shrink
                    mixed = mixed + acc[:, chunk] * shrink
                top[:, chunk] = high
                total[:, chunk] = part
                acc[:, chunk] = mixed

    def finish(half):
        part = slice(half * half_rows, (half + 1) * half_rows)
        result = (acc[:, part] / total[:, part]).T.astype(jnp.bfloat16)
        leaving[2 * half:2 * half + 2] = result.reshape(2, per_group, tokens, HD)

    for which in (0, 1):
        for r in range(3):
            piece(which, r).start()
    for r in range(3):
        queries_out(r).start()
    prepare_bias()
    column(0)
    local_copies[2].wait()
    prepare_rows(3, chip)
    for r in range(3):
        queries_out(r).wait_recv()
        prepare_rows(r, away[r])
    q_ext[...] = q_rows[...].T
    column(1)
    beside(0)
    mine = pl.ds(chip * per_group, per_group)
    keep = pltpu.make_async_copy(leaving.at[3], done.at[mine], local_sems.at[4])
    for k in range(4):
        attend(k, 0)
        if k < 2:
            column(k + 2)

        @pl.when(z == k)
        def _():
            finish(0)
            result_home(0).start()
            result_home(1).start()

        attend(k, 1)

        @pl.when(z == k)
        def _():
            finish(1)
            result_home(2).start()
            keep.start()

        if k < 3:
            beside(k + 1)

    for which in (0, 1):
        for r in range(3):
            piece(which, r).wait_send()
    for r in range(3):
        queries_out(r).wait_send()
    for k in range(4):
        sent(k)
    keep.wait()
    for r in range(3):
        result_arrived(r)
    for place in range(H):
        out_ref[:, place * HD:(place + 1) * HD] = done[order_ref[place]]
    for r in range(3):
        result_home(r).wait_send()


def planes_local(queries, keys, values, block_index, block_count, head_order):
    tokens = queries.shape[0]
    planes = lax.axis_size("head")
    per_group = H // KVH
    rows = 4 * per_group * tokens
    table = block_index.transpose(0, 2, 1)
    any_spec = pl.BlockSpec(memory_space=pl.ANY)
    return pl.pallas_call(
        plane_kernel,
        out_shape=jax.ShapeDtypeStruct(queries.shape, jnp.bfloat16),
        in_specs=[any_spec] * 4 + [pl.BlockSpec(memory_space=pltpu.SMEM)],
        out_specs=pl.BlockSpec(memory_space=pltpu.VMEM),
        scratch_shapes=[
            pltpu.VMEM((planes * 2, 4 * tokens, HD), jnp.bfloat16),
            pltpu.VMEM((planes * 2, 4 * tokens, HD), jnp.bfloat16),
            pltpu.VMEM((4, tokens, per_group * HD), jnp.bfloat16),
            pltpu.VMEM((rows, 2 * HD), jnp.bfloat16),
            pltpu.VMEM((2 * HD, rows), jnp.bfloat16),
            pltpu.VMEM((HD, rows), jnp.float32),
            pltpu.VMEM((1, rows), jnp.float32),
            pltpu.VMEM((1, rows), jnp.float32),
            pltpu.VMEM((4,) + table.shape[1:], jnp.int32),
            pltpu.VMEM((HD, HD), jnp.float32),
            pltpu.VMEM((4, HD, HD), jnp.float32),
            pltpu.VMEM((H, tokens, HD), jnp.bfloat16),
            pltpu.VMEM((4, per_group, tokens, HD), jnp.bfloat16),
            pltpu.SemaphoreType.DMA((5,)),
            pltpu.SemaphoreType.DMA((2, 3)),
            pltpu.SemaphoreType.DMA((2, 3)),
            pltpu.SemaphoreType.DMA((2, 3)),
            pltpu.SemaphoreType.DMA((2, 3)),
            pltpu.SemaphoreType.DMA((planes, 4)),
            pltpu.SemaphoreType.DMA((planes, 2, 2)),
        ],
        compiler_params=pltpu.CompilerParams(
            collective_id=0, has_side_effects=True, vmem_limit_bytes=60 * 1024 * 1024
        ),
    )(queries, keys, values, table, head_order)


def solution(mesh):
    in_planes = mesh.shape["head"] == 4 and mesh.shape["ctx"] == 8
    return jax.shard_map(
        planes_local if in_planes else local,
        mesh=mesh,
        in_specs=(
            P(("head", "ctx"), None),
            P(("head", "ctx"), None),
            P(("head", "ctx"), None),
            P(),
            P(),
            P(),
        ),
        out_specs=P(("head", "ctx"), None),
        check_vma=False,
    )
```

```python
from functools import partial
import math

import jax
import jax.numpy as jnp
from jax import lax
from jax.experimental import pallas as pl
from jax.experimental.pallas import tpu as pltpu
from jax.sharding import PartitionSpec as P

H = 28
KVH = 4
HD = 128
BLOCK = 128


FLOOR = -1e30
MESH = pl.DeviceIdType.MESH


def positions(stripes, stripe_len, device, ctx_total):
    offsets = jnp.arange(stripes * stripe_len, dtype=jnp.int32)
    stripe = offsets // stripe_len
    return (stripe * ctx_total + device) * stripe_len + offsets % stripe_len


def keep_state(carried):
    return carried


def update_lanes(query_rows, key_lanes, value_lanes, allowed, score_scale, carried):
    running_max, running_sum, running_out = carried
    scores = (
        jnp.einsum("qgd,kgd->qgk", query_rows, key_lanes, preferred_element_type=jnp.float32)
        * score_scale
    )
    scores = jnp.where(allowed, scores, FLOOR)
    new_max = jnp.maximum(running_max, jnp.max(scores, axis=2))
    weights = jnp.where(allowed, jnp.exp(scores - new_max[:, :, None]), 0.0)
    factor = jnp.exp(running_max - new_max)
    new_sum = running_sum * factor + jnp.sum(weights, axis=2)
    update = jnp.einsum(
        "qgk,kgd->qgd",
        weights.astype(jnp.bfloat16),
        value_lanes,
        preferred_element_type=jnp.float32,
    )
    new_out = running_out * factor[:, :, None] + update
    return (new_max, new_sum, new_out)


def local(queries, keys, values, block_index, block_count, head_order):
    local_tokens = queries.shape[0]
    per_group = H // KVH
    head_total = lax.axis_size("head")
    ctx_total = lax.axis_size("ctx")
    ctx_here = lax.axis_index("ctx")
    head_here = lax.axis_index("head")
    query_split = queries.reshape(local_tokens, H, HD)
    key_split = keys.reshape(local_tokens, KVH, HD)
    value_split = values.reshape(local_tokens, KVH, HD)
    query_sorted = jnp.take(query_split, head_order, axis=1)
    kv_lists = (head_order // per_group).reshape(head_total, per_group)
    kv_pairs = jnp.stack([jnp.min(kv_lists, axis=1), jnp.max(kv_lists, axis=1)], axis=1).reshape(
        head_total * 2
    )
    key_sent = jnp.take(key_split, kv_pairs, axis=1).reshape(local_tokens, head_total, 2, HD)
    value_sent = jnp.take(value_split, kv_pairs, axis=1).reshape(local_tokens, head_total, 2, HD)
    own_heads = lax.dynamic_slice_in_dim(head_order, head_here * per_group, per_group)
    own_kv = own_heads // per_group
    slot_of = (own_kv == jnp.max(own_kv)).astype(jnp.int32)
    query_sent = query_sorted.reshape(local_tokens, head_total, per_group, HD)
    query_got, key_got, value_got = (
        lax.all_to_all(query_sent, "head", split_axis=1, concat_axis=0, tiled=True),
        lax.all_to_all(key_sent, "head", split_axis=1, concat_axis=0, tiled=True),
        lax.all_to_all(value_sent, "head", split_axis=1, concat_axis=0, tiled=True),
    )
    row_count = head_total * local_tokens
    slot_count = key_sent.shape[2]
    query_rows = query_got.reshape(row_count, per_group, HD)
    key_rows = key_got.reshape(row_count, slot_count, HD)
    value_rows = value_got.reshape(row_count, slot_count, HD)
    query_pos = positions(head_total, local_tokens, ctx_here, ctx_total)
    per_entry = min(local_tokens, BLOCK)
    entries = row_count // per_entry
    entry_blocks = query_pos[::per_entry] // BLOCK
    block_total = block_index.shape[2]
    block_iota = jnp.arange(block_total, dtype=jnp.int32)
    listed = jnp.take(jnp.take(block_index, entry_blocks, axis=0), own_heads, axis=1)
    counted = jnp.take(jnp.take(block_count, entry_blocks, axis=0), own_heads, axis=1)
    usable = block_iota[None, None, :] < counted[:, :, None]
    block_hits = (listed[:, :, :, None] == block_iota[None, None, None, :]) & usable[:, :, :, None]
    table_flags = jnp.any(block_hits, axis=2).astype(jnp.bfloat16)
    score_scale = 1.0 / math.sqrt(HD)
    initial = (
        jnp.full((row_count, per_group), FLOOR, jnp.float32),
        jnp.zeros((row_count, per_group), jnp.float32),
        jnp.zeros((row_count, per_group, HD), jnp.float32),
    )
    key_piece = lax.all_gather(key_rows, "ctx", axis=0, tiled=True)
    value_piece = lax.all_gather(value_rows, "ctx", axis=0, tiled=True)
    shard_total = key_piece.shape[0] // row_count

    def one_shard(number, inner_state):
        key_block = lax.dynamic_slice_in_dim(key_piece, number * row_count, row_count, 0)
        value_block = lax.dynamic_slice_in_dim(value_piece, number * row_count, row_count, 0)
        key_lanes = jnp.take(key_block, slot_of, axis=1)
        value_lanes = jnp.take(value_block, slot_of, axis=1)
        key_pos = positions(head_total, local_tokens, number, ctx_total)
        onehot = (block_iota[:, None] == (key_pos // BLOCK)[None, :]).astype(jnp.bfloat16)
        chosen = jnp.einsum("egb,bk->egk", table_flags, onehot, preferred_element_type=jnp.float32)
        spread = jnp.broadcast_to(
            chosen[:, None], (entries, per_entry, per_group, row_count)
        ).reshape(row_count, per_group, row_count)
        allowed = (spread > 0.5) & (key_pos[None, None, :] <= query_pos[:, None, None])
        return lax.cond(
            jnp.any(allowed),
            partial(update_lanes, query_rows, key_lanes, value_lanes, allowed, score_scale),
            keep_state,
            inner_state,
        )

    folded = lax.fori_loop(0, shard_total, one_shard, initial)
    running_max, running_sum, running_out = folded
    attended = (
        (running_out / running_sum[:, :, None])
        .astype(jnp.bfloat16)
        .reshape(row_count, 1, per_group, HD)
    )
    returned = lax.all_to_all(attended, "head", split_axis=0, concat_axis=1, tiled=True).reshape(
        local_tokens, H, HD
    )
    return returned.reshape(local_tokens, H * HD)


MASKED = -1e30


def plane_kernel(
    q_ref, k_ref, v_ref, table_ref, order_ref, out_ref,
    k_all, v_all, q_in, q_rows, q_ext, acc, top, total, lists, bias_by_block,
    bias_by_head, done, leaving, local_sems, piece_send, piece_recv, head_send, head_recv,
    send_sems, recv_sems,
):
    z = lax.axis_index("head")
    ctx = lax.axis_index("ctx")
    planes = lax.axis_size("head")
    tokens = q_ref.shape[0]
    per_group = H // KVH
    width = per_group * HD
    rows = 4 * per_group * tokens
    lane_keys = 4 * tokens
    core = ctx % 2
    other = 1 - core
    chip = ctx // 2
    x_chip = chip + 1 - 2 * (chip % 2)
    y_chip = chip + 2 - 4 * (chip // 2)
    d_chip = x_chip + y_chip - chip
    away = (y_chip, x_chip, d_chip)
    slots = (0, 2, 3)
    sib = 2 * chip + other
    bufs = (k_all, v_all)
    heres = (k_ref, v_ref)

    def head_columns(of_chip, size):
        return pl.ds(pl.multiple_of(of_chip * size, size), size)

    def chip_rows(of_chip):
        return pl.ds(pl.multiple_of(of_chip * tokens, tokens), tokens)

    own_places = [bufs[which].at[z * 2 + core, chip_rows(chip)] for which in (0, 1)]
    local_copies = [
        pltpu.make_async_copy(
            heres[which].at[:, head_columns(chip, HD)], own_places[which], local_sems.at[which]
        )
        for which in (0, 1)
    ]
    local_copies.append(pltpu.make_async_copy(
        q_ref.at[:, head_columns(chip, width)], q_in.at[1], local_sems.at[2]
    ))
    local_copies.append(pltpu.make_async_copy(
        table_ref.at[pl.ds(z * 4, 4)], lists, local_sems.at[3]
    ))
    for copy in local_copies:
        copy.start()

    barrier = pltpu.get_barrier_semaphore()

    def greet(head_to, ctx_to):
        pl.semaphore_signal(
            barrier, inc=1, device_id={"head": head_to, "ctx": ctx_to}, device_id_type=MESH
        )

    greet(z, sib)
    for near in away:
        greet(z, 2 * near + core)

    @pl.when(z > 0)
    def _():
        greet(z - 1, ctx)

    @pl.when(z < planes - 1)
    def _():
        greet(z + 1, ctx)

    pl.semaphore_wait(
        barrier, 4 + (z > 0).astype(jnp.int32) + (z < planes - 1).astype(jnp.int32)
    )

    def remote(src, dst, send_sem, recv_sem, head_to, ctx_to):
        return pltpu.make_async_remote_copy(
            src_ref=src,
            dst_ref=dst,
            send_sem=send_sem,
            recv_sem=recv_sem,
            device_id={"head": head_to, "ctx": ctx_to},
            device_id_type=MESH,
        )

    def piece(which, r):
        return remote(
            heres[which].at[:, head_columns(away[r], HD)],
            own_places[which],
            piece_send.at[which, r],
            piece_recv.at[which, r],
            z, 2 * away[r] + core,
        )

    def piece_arrived(which, r):
        place = bufs[which].at[z * 2 + core, chip_rows(away[r])]
        remote(
            place, place, piece_send.at[which, r], piece_recv.at[which, r], z, sib
        ).wait_recv()

    def queries_out(r):
        return remote(
            q_ref.at[:, head_columns(away[r], width)],
            q_in.at[slots[r]],
            head_send.at[0, r],
            head_recv.at[0, r],
            z, 2 * away[r] + core,
        )

    def result_home(r):
        return remote(
            leaving.at[slots[r]],
            done.at[pl.ds(chip * per_group, per_group)],
            head_send.at[1, r],
            head_recv.at[1, r],
            z, 2 * away[r] + core,
        )

    def result_arrived(r):
        remote(
            leaving.at[slots[r]],
            done.at[pl.ds(away[r] * per_group, per_group)],
            head_send.at[1, r],
            head_recv.at[1, r],
            z, sib,
        ).wait_recv()

    def whole(which, k, lane, kind, head_to, ctx_to):
        place = bufs[which].at[(z - k) * 2 + lane]
        return remote(
            place, place, send_sems.at[k, kind], recv_sems.at[z - k, lane, which],
            head_to, ctx_to,
        )

    def column(k):
        @pl.when(z >= k)
        def _():
            for which in (0, 1):
                if k == 0:
                    local_copies[which].wait()
                    for r in range(3):
                        piece_arrived(which, r)
                else:
                    whole(which, k, core, 0, z, sib).wait_recv()

                @pl.when(z < planes - 1)
                def _():
                    whole(which, k, core, which, z + 1, ctx).start()

                whole(which, k, core, 2 + which, z, sib).start()

    def beside(k):
        @pl.when(z >= k)
        def _():
            for which in (0, 1):
                whole(which, k, other, 0, z, sib).wait_recv()

    def sent(k):
        @pl.when(z >= k)
        def _():
            @pl.when(z < planes - 1)
            def _():
                for kind in (0, 1):
                    whole(0, k, core, kind, z, sib).wait_send()

            for kind in (2, 3):
                whole(0, k, core, kind, z, sib).wait_send()

    def prepare_bias():
        local_copies[3].wait()
        listed = lists[...]
        entries = listed.shape[1]
        spot = lax.broadcasted_iota(jnp.int32, listed.shape, 1)
        query_block = z * 4 + lax.broadcasted_iota(jnp.int32, listed.shape, 0)
        last = jnp.min(jnp.where(listed == query_block, spot, entries), axis=1, keepdims=True)
        listed = jnp.where(spot <= last, listed, -1)
        bias_by_block[...] = jnp.zeros_like(bias_by_block)
        for chip_here in range(4):
            block = lax.broadcasted_iota(jnp.int32, (entries, H), 0)
            bias = jnp.full((entries, H), MASKED, jnp.float32)
            for e in range(entries):
                bias = jnp.where(listed[chip_here, e:e + 1, :] == block, 0.0, bias)
            bias_by_block[:entries, :H] = bias
            bias_by_head[chip_here] = bias_by_block[...].T

    def prepare_rows(r, of_chip):
        for g in range(per_group):
            row = (r * per_group + g) * tokens
            q_rows[row:row + tokens, :HD] = q_in[r, :, g * HD:(g + 1) * HD]
            q_rows[row:row + tokens, HD:] = jnp.broadcast_to(
                bias_by_head[of_chip, pl.ds(chip * per_group + g, 1), :], (tokens, HD)
            ).astype(jnp.bfloat16)

    keys_here = 2 * lane_keys
    half_rows = rows // 2
    scale = 1.0 / math.sqrt(HD)
    starts = range(0, half_rows, 2 * HD)
    chunks = [
        [slice(h * half_rows + i, h * half_rows + min(i + 2 * HD, half_rows)) for i in starts]
        for h in (0, 1)
    ]

    def attend(k, half):
        @pl.when(z >= k)
        def _():
            plane = z - k
            key_row = lax.broadcasted_iota(jnp.int32, (keys_here, HD), 0)
            key_lane = lax.broadcasted_iota(jnp.int32, (keys_here, HD), 1)
            block_of = plane * 4 + key_row % lane_keys // tokens
            onehot = jnp.where(block_of == key_lane, 1.0, 0.0).astype(jnp.bfloat16)
            key = k_all[pl.ds(plane * 2, 2)].reshape(keys_here, HD)
            value = v_all[pl.ds(plane * 2, 2)].reshape(keys_here, HD).T
            key = jnp.concatenate([key, onehot], axis=1)
            for chunk in chunks[half]:
                s = jnp.dot(key, q_ext[:, chunk], preferred_element_type=jnp.float32)
                if k == 0:
                    key_at = lax.broadcasted_iota(jnp.int32, (keys_here, 1), 0)
                    key_pos = (
                        key_at % lane_keys // tokens * 2 + key_at // lane_keys
                    ) * tokens + key_at % tokens
                    row_at = chunk.start + lax.broadcasted_iota(
                        jnp.int32, (1, chunk.stop - chunk.start), 1
                    )
                    source = row_at // (per_group * tokens)
                    row_chip = jnp.where(
                        source == 0, y_chip,
                        jnp.where(source == 1, chip, jnp.where(source == 2, x_chip, d_chip)),
                    )
                    row_pos = (row_chip * 2 + core) * tokens + row_at % tokens
                    s = jnp.where(key_pos <= row_pos, s, MASKED)
                high = jnp.max(s, axis=0, keepdims=True)
                if k > 0:
                    old = top[:, chunk]
                    high = jnp.maximum(high, old)
                    shrink = jnp.exp((old - high) * scale)
                w = jnp.exp((s - high) * scale)
                part = jnp.sum(w, axis=0, keepdims=True)
                mixed = jnp.dot(value, w.astype(jnp.bfloat16), preferred_element_type=jnp.float32)
                if k > 0:
                    part = part + total[:, chunk] * shrink
                    mixed = mixed + acc[:, chunk] * shrink
                top[:, chunk] = high
                total[:, chunk] = part
                acc[:, chunk] = mixed

    def finish(half):
        part = slice(half * half_rows, (half + 1) * half_rows)
        result = (acc[:, part] / total[:, part]).T.astype(jnp.bfloat16)
        leaving[2 * half:2 * half + 2] = result.reshape(2, per_group, tokens, HD)

    mine = pl.ds(chip * per_group, per_group)
    keep = pltpu.make_async_copy(leaving.at[1], done.at[mine], local_sems.at[4])

    def turn_rows(half):
        part = slice(half * half_rows, (half + 1) * half_rows)
        q_ext[:, part] = q_rows[part, :].T

    def send_half(half):
        if half == 0:
            result_home(0).start()
            keep.start()
        else:
            result_home(2).start()
            result_home(1).start()

    for which in (0, 1):
        for r in range(3):
            piece(which, r).start()
    prepare_bias()
    for r in (2, 0, 1):
        queries_out(r).start()
    column(0)
    local_copies[2].wait()
    prepare_rows(1, chip)
    queries_out(0).wait_recv()
    prepare_rows(0, y_chip)
    turn_rows(0)
    column(1)
    beside(0)
    attend(0, 0)
    for r in (1, 2):
        queries_out(r).wait_recv()
        prepare_rows(slots[r], away[r])
    turn_rows(1)
    attend(0, 1)

    @pl.when(z == 0)
    def _():
        finish(0)
        finish(1)
        send_half(1)
        send_half(0)

    for k in range(1, 4):
        if k == 1:
            column(2)
        beside(k)
        attend(k, 1)
        if k == 2:
            column(3)

        @pl.when(z == k)
        def _():
            finish(1)
            send_half(1)

        attend(k, 0)

        @pl.when(z == k)
        def _():
            finish(0)
            send_half(0)

    for which in (0, 1):
        for r in range(3):
            piece(which, r).wait_send()
    for r in range(3):
        queries_out(r).wait_send()
    for k in range(4):
        sent(k)
    keep.wait()
    for r in range(3):
        result_arrived(r)
    for place in range(H):
        out_ref[:, place * HD:(place + 1) * HD] = done[order_ref[place]]
    for r in range(3):
        result_home(r).wait_send()


def planes_local(queries, keys, values, block_index, block_count, head_order):
    tokens = queries.shape[0]
    planes = lax.axis_size("head")
    per_group = H // KVH
    rows = 4 * per_group * tokens
    table = block_index.transpose(0, 2, 1)
    any_spec = pl.BlockSpec(memory_space=pl.ANY)
    return pl.pallas_call(
        plane_kernel,
        out_shape=jax.ShapeDtypeStruct(queries.shape, jnp.bfloat16),
        in_specs=[any_spec] * 4 + [pl.BlockSpec(memory_space=pltpu.SMEM)],
        out_specs=pl.BlockSpec(memory_space=pltpu.VMEM),
        scratch_shapes=[
            pltpu.VMEM((planes * 2, 4 * tokens, HD), jnp.bfloat16),
            pltpu.VMEM((planes * 2, 4 * tokens, HD), jnp.bfloat16),
            pltpu.VMEM((4, tokens, per_group * HD), jnp.bfloat16),
            pltpu.VMEM((rows, 2 * HD), jnp.bfloat16),
            pltpu.VMEM((2 * HD, rows), jnp.bfloat16),
            pltpu.VMEM((HD, rows), jnp.float32),
            pltpu.VMEM((1, rows), jnp.float32),
            pltpu.VMEM((1, rows), jnp.float32),
            pltpu.VMEM((4,) + table.shape[1:], jnp.int32),
            pltpu.VMEM((HD, HD), jnp.float32),
            pltpu.VMEM((4, HD, HD), jnp.float32),
            pltpu.VMEM((H, tokens, HD), jnp.bfloat16),
            pltpu.VMEM((4, per_group, tokens, HD), jnp.bfloat16),
            pltpu.SemaphoreType.DMA((5,)),
            pltpu.SemaphoreType.DMA((2, 3)),
            pltpu.SemaphoreType.DMA((2, 3)),
            pltpu.SemaphoreType.DMA((2, 3)),
            pltpu.SemaphoreType.DMA((2, 3)),
            pltpu.SemaphoreType.DMA((planes, 4)),
            pltpu.SemaphoreType.DMA((planes, 2, 2)),
        ],
        compiler_params=pltpu.CompilerParams(
            collective_id=0, has_side_effects=True, vmem_limit_bytes=60 * 1024 * 1024
        ),
    )(queries, keys, values, table, head_order)


def solution(mesh):
    in_planes = mesh.shape["head"] == 4 and mesh.shape["ctx"] == 8
    return jax.shard_map(
        planes_local if in_planes else local,
        mesh=mesh,
        in_specs=(
            P(("head", "ctx"), None),
            P(("head", "ctx"), None),
            P(("head", "ctx"), None),
            P(),
            P(),
            P(),
        ),
        out_specs=P(("head", "ctx"), None),
        check_vma=False,
    )
```

```python
from functools import partial
import math

import jax
import jax.numpy as jnp
from jax import lax
from jax.experimental import pallas as pl
from jax.experimental.pallas import tpu as pltpu
from jax.sharding import PartitionSpec as P

H = 28
KVH = 4
HD = 128
BLOCK = 128


FLOOR = -1e30
MESH = pl.DeviceIdType.MESH


def positions(stripes, stripe_len, device, ctx_total):
    offsets = jnp.arange(stripes * stripe_len, dtype=jnp.int32)
    stripe = offsets // stripe_len
    return (stripe * ctx_total + device) * stripe_len + offsets % stripe_len


def keep_state(carried):
    return carried


def update_lanes(query_rows, key_lanes, value_lanes, allowed, score_scale, carried):
    running_max, running_sum, running_out = carried
    scores = (
        jnp.einsum("qgd,kgd->qgk", query_rows, key_lanes, preferred_element_type=jnp.float32)
        * score_scale
    )
    scores = jnp.where(allowed, scores, FLOOR)
    new_max = jnp.maximum(running_max, jnp.max(scores, axis=2))
    weights = jnp.where(allowed, jnp.exp(scores - new_max[:, :, None]), 0.0)
    factor = jnp.exp(running_max - new_max)
    new_sum = running_sum * factor + jnp.sum(weights, axis=2)
    update = jnp.einsum(
        "qgk,kgd->qgd",
        weights.astype(jnp.bfloat16),
        value_lanes,
        preferred_element_type=jnp.float32,
    )
    new_out = running_out * factor[:, :, None] + update
    return (new_max, new_sum, new_out)


def local(queries, keys, values, block_index, block_count, head_order):
    local_tokens = queries.shape[0]
    per_group = H // KVH
    head_total = lax.axis_size("head")
    ctx_total = lax.axis_size("ctx")
    ctx_here = lax.axis_index("ctx")
    head_here = lax.axis_index("head")
    query_split = queries.reshape(local_tokens, H, HD)
    key_split = keys.reshape(local_tokens, KVH, HD)
    value_split = values.reshape(local_tokens, KVH, HD)
    query_sorted = jnp.take(query_split, head_order, axis=1)
    kv_lists = (head_order // per_group).reshape(head_total, per_group)
    kv_pairs = jnp.stack([jnp.min(kv_lists, axis=1), jnp.max(kv_lists, axis=1)], axis=1).reshape(
        head_total * 2
    )
    key_sent = jnp.take(key_split, kv_pairs, axis=1).reshape(local_tokens, head_total, 2, HD)
    value_sent = jnp.take(value_split, kv_pairs, axis=1).reshape(local_tokens, head_total, 2, HD)
    own_heads = lax.dynamic_slice_in_dim(head_order, head_here * per_group, per_group)
    own_kv = own_heads // per_group
    slot_of = (own_kv == jnp.max(own_kv)).astype(jnp.int32)
    query_sent = query_sorted.reshape(local_tokens, head_total, per_group, HD)
    query_got, key_got, value_got = (
        lax.all_to_all(query_sent, "head", split_axis=1, concat_axis=0, tiled=True),
        lax.all_to_all(key_sent, "head", split_axis=1, concat_axis=0, tiled=True),
        lax.all_to_all(value_sent, "head", split_axis=1, concat_axis=0, tiled=True),
    )
    row_count = head_total * local_tokens
    slot_count = key_sent.shape[2]
    query_rows = query_got.reshape(row_count, per_group, HD)
    key_rows = key_got.reshape(row_count, slot_count, HD)
    value_rows = value_got.reshape(row_count, slot_count, HD)
    query_pos = positions(head_total, local_tokens, ctx_here, ctx_total)
    per_entry = min(local_tokens, BLOCK)
    entries = row_count // per_entry
    entry_blocks = query_pos[::per_entry] // BLOCK
    block_total = block_index.shape[2]
    block_iota = jnp.arange(block_total, dtype=jnp.int32)
    listed = jnp.take(jnp.take(block_index, entry_blocks, axis=0), own_heads, axis=1)
    counted = jnp.take(jnp.take(block_count, entry_blocks, axis=0), own_heads, axis=1)
    usable = block_iota[None, None, :] < counted[:, :, None]
    block_hits = (listed[:, :, :, None] == block_iota[None, None, None, :]) & usable[:, :, :, None]
    table_flags = jnp.any(block_hits, axis=2).astype(jnp.bfloat16)
    score_scale = 1.0 / math.sqrt(HD)
    initial = (
        jnp.full((row_count, per_group), FLOOR, jnp.float32),
        jnp.zeros((row_count, per_group), jnp.float32),
        jnp.zeros((row_count, per_group, HD), jnp.float32),
    )
    key_piece = lax.all_gather(key_rows, "ctx", axis=0, tiled=True)
    value_piece = lax.all_gather(value_rows, "ctx", axis=0, tiled=True)
    shard_total = key_piece.shape[0] // row_count

    def one_shard(number, inner_state):
        key_block = lax.dynamic_slice_in_dim(key_piece, number * row_count, row_count, 0)
        value_block = lax.dynamic_slice_in_dim(value_piece, number * row_count, row_count, 0)
        key_lanes = jnp.take(key_block, slot_of, axis=1)
        value_lanes = jnp.take(value_block, slot_of, axis=1)
        key_pos = positions(head_total, local_tokens, number, ctx_total)
        onehot = (block_iota[:, None] == (key_pos // BLOCK)[None, :]).astype(jnp.bfloat16)
        chosen = jnp.einsum("egb,bk->egk", table_flags, onehot, preferred_element_type=jnp.float32)
        spread = jnp.broadcast_to(
            chosen[:, None], (entries, per_entry, per_group, row_count)
        ).reshape(row_count, per_group, row_count)
        allowed = (spread > 0.5) & (key_pos[None, None, :] <= query_pos[:, None, None])
        return lax.cond(
            jnp.any(allowed),
            partial(update_lanes, query_rows, key_lanes, value_lanes, allowed, score_scale),
            keep_state,
            inner_state,
        )

    folded = lax.fori_loop(0, shard_total, one_shard, initial)
    running_max, running_sum, running_out = folded
    attended = (
        (running_out / running_sum[:, :, None])
        .astype(jnp.bfloat16)
        .reshape(row_count, 1, per_group, HD)
    )
    returned = lax.all_to_all(attended, "head", split_axis=0, concat_axis=1, tiled=True).reshape(
        local_tokens, H, HD
    )
    return returned.reshape(local_tokens, H * HD)


MASKED = -1e30


def plane_kernel(
    q_ref, k_ref, v_ref, table_ref, order_ref, out_ref,
    k_all, v_all, q_in, q_rows, q_ext, acc, top, total, lists, bias_by_block,
    bias_by_head, done, leaving, local_sems, piece_send, piece_recv, head_send, head_recv,
    send_sems, recv_sems,
):
    z = lax.axis_index("head")
    ctx = lax.axis_index("ctx")
    planes = lax.axis_size("head")
    tokens = q_ref.shape[0]
    per_group = H // KVH
    width = per_group * HD
    rows = 4 * per_group * tokens
    lane_keys = 4 * tokens
    core = ctx % 2
    other = 1 - core
    chip = ctx // 2
    x_chip = chip + 1 - 2 * (chip % 2)
    y_chip = chip + 2 - 4 * (chip // 2)
    d_chip = x_chip + y_chip - chip
    away = (y_chip, x_chip, d_chip)
    slots = (0, 2, 3)
    sib = 2 * chip + other
    bufs = (k_all, v_all)
    heres = (k_ref, v_ref)

    def head_columns(of_chip, size):
        return pl.ds(pl.multiple_of(of_chip * size, size), size)

    def chip_rows(of_chip):
        return pl.ds(pl.multiple_of(of_chip * tokens, tokens), tokens)

    own_places = [bufs[which].at[z * 2 + core, chip_rows(chip)] for which in (0, 1)]
    local_copies = [
        pltpu.make_async_copy(
            heres[which].at[:, head_columns(chip, HD)], own_places[which], local_sems.at[which]
        )
        for which in (0, 1)
    ]
    local_copies.append(pltpu.make_async_copy(
        q_ref.at[:, head_columns(chip, width)], q_in.at[1], local_sems.at[2]
    ))
    local_copies.append(pltpu.make_async_copy(
        table_ref.at[pl.ds(z * 4, 4)], lists, local_sems.at[3]
    ))
    for copy in local_copies:
        copy.start()

    barrier = pltpu.get_barrier_semaphore()

    def greet(head_to, ctx_to):
        pl.semaphore_signal(
            barrier, inc=1, device_id={"head": head_to, "ctx": ctx_to}, device_id_type=MESH
        )

    greet(z, sib)
    for near in away:
        greet(z, 2 * near + core)

    @pl.when(z > 0)
    def _():
        greet(z - 1, ctx)

    @pl.when(z < planes - 1)
    def _():
        greet(z + 1, ctx)

    pl.semaphore_wait(
        barrier, 4 + (z > 0).astype(jnp.int32) + (z < planes - 1).astype(jnp.int32)
    )

    def remote(src, dst, send_sem, recv_sem, head_to, ctx_to):
        return pltpu.make_async_remote_copy(
            src_ref=src,
            dst_ref=dst,
            send_sem=send_sem,
            recv_sem=recv_sem,
            device_id={"head": head_to, "ctx": ctx_to},
            device_id_type=MESH,
        )

    def piece(which, r):
        return remote(
            heres[which].at[:, head_columns(away[r], HD)],
            own_places[which],
            piece_send.at[which, r],
            piece_recv.at[which, r],
            z, 2 * away[r] + core,
        )

    def piece_arrived(which, r):
        place = bufs[which].at[z * 2 + core, chip_rows(away[r])]
        remote(
            place, place, piece_send.at[which, r], piece_recv.at[which, r], z, sib
        ).wait_recv()

    def queries_out(r):
        return remote(
            q_ref.at[:, head_columns(away[r], width)],
            q_in.at[slots[r]],
            head_send.at[0, r],
            head_recv.at[0, r],
            z, 2 * away[r] + core,
        )

    def result_home(r):
        return remote(
            leaving.at[slots[r]],
            done.at[pl.ds(chip * per_group, per_group)],
            head_send.at[1, r],
            head_recv.at[1, r],
            z, 2 * away[r] + core,
        )

    def result_arrived(r):
        remote(
            leaving.at[slots[r]],
            done.at[pl.ds(away[r] * per_group, per_group)],
            head_send.at[1, r],
            head_recv.at[1, r],
            z, sib,
        ).wait_recv()

    def whole(which, k, lane, kind, head_to, ctx_to):
        place = bufs[which].at[(z - k) * 2 + lane]
        return remote(
            place, place, send_sems.at[k, kind], recv_sems.at[z - k, lane, which],
            head_to, ctx_to,
        )

    def column(k):
        @pl.when(z >= k)
        def _():
            for which in (0, 1):
                if k == 0:
                    local_copies[which].wait()
                    for r in range(3):
                        piece_arrived(which, r)
                else:
                    whole(which, k, core, 0, z, sib).wait_recv()

                @pl.when(z < planes - 1)
                def _():
                    whole(which, k, core, which, z + 1, ctx).start()

                whole(which, k, core, 2 + which, z, sib).start()

    def beside(k):
        @pl.when(z >= k)
        def _():
            for which in (0, 1):
                whole(which, k, other, 0, z, sib).wait_recv()

    def sent(k):
        @pl.when(z >= k)
        def _():
            @pl.when(z < planes - 1)
            def _():
                for kind in (0, 1):
                    whole(0, k, core, kind, z, sib).wait_send()

            for kind in (2, 3):
                whole(0, k, core, kind, z, sib).wait_send()

    def prepare_bias():
        local_copies[3].wait()
        listed = lists[...]
        entries = listed.shape[1]
        spot = lax.broadcasted_iota(jnp.int32, listed.shape, 1)
        query_block = z * 4 + lax.broadcasted_iota(jnp.int32, listed.shape, 0)
        last = jnp.min(jnp.where(listed == query_block, spot, entries), axis=1, keepdims=True)
        listed = jnp.where(spot <= last, listed, -1)
        bias_by_block[...] = jnp.zeros_like(bias_by_block)
        for chip_here in range(4):
            block = lax.broadcasted_iota(jnp.int32, (entries, H), 0)
            bias = jnp.full((entries, H), MASKED, jnp.float32)
            for e in range(entries):
                bias = jnp.where(listed[chip_here, e:e + 1, :] == block, 0.0, bias)
            bias_by_block[:entries, :H] = bias
            bias_by_head[chip_here] = bias_by_block[...].T

    def prepare_rows(r, of_chip):
        for g in range(per_group):
            row = (r * per_group + g) * tokens
            q_rows[row:row + tokens, :HD] = q_in[r, :, g * HD:(g + 1) * HD]
            q_rows[row:row + tokens, HD:] = jnp.broadcast_to(
                bias_by_head[of_chip, pl.ds(chip * per_group + g, 1), :], (tokens, HD)
            ).astype(jnp.bfloat16)

    keys_here = 2 * lane_keys
    half_rows = rows // 2
    scale = 1.0 / math.sqrt(HD)
    starts = range(0, half_rows, 2 * HD)
    chunks = [
        [slice(h * half_rows + i, h * half_rows + min(i + 2 * HD, half_rows)) for i in starts]
        for h in (0, 1)
    ]

    def attend(k, halves):
        @pl.when(z >= k)
        def _():
            plane = z - k
            key_row = lax.broadcasted_iota(jnp.int32, (keys_here, HD), 0)
            key_lane = lax.broadcasted_iota(jnp.int32, (keys_here, HD), 1)
            block_of = plane * 4 + key_row % lane_keys // tokens
            onehot = jnp.where(block_of == key_lane, 1.0, 0.0).astype(jnp.bfloat16)
            key = k_all[pl.ds(plane * 2, 2)].reshape(keys_here, HD)
            value = v_all[pl.ds(plane * 2, 2)].reshape(keys_here, HD).T
            key = jnp.concatenate([key, onehot], axis=1)
            todo = [chunk for half in halves for chunk in chunks[half]]

            def score(chunk):
                return jnp.dot(key, q_ext[:, chunk], preferred_element_type=jnp.float32)

            def weigh(chunk, s):
                if k == 0:
                    key_at = lax.broadcasted_iota(jnp.int32, (keys_here, 1), 0)
                    key_pos = (
                        key_at % lane_keys // tokens * 2 + key_at // lane_keys
                    ) * tokens + key_at % tokens
                    row_at = chunk.start + lax.broadcasted_iota(
                        jnp.int32, (1, chunk.stop - chunk.start), 1
                    )
                    source = row_at // (per_group * tokens)
                    row_chip = jnp.where(
                        source == 0, y_chip,
                        jnp.where(source == 1, chip, jnp.where(source == 2, x_chip, d_chip)),
                    )
                    row_pos = (row_chip * 2 + core) * tokens + row_at % tokens
                    s = jnp.where(key_pos <= row_pos, s, MASKED)
                high = jnp.max(s, axis=0, keepdims=True)
                shrink = None
                if k > 0:
                    old = top[:, chunk]
                    high = jnp.maximum(high, old)
                    shrink = jnp.exp((old - high) * scale)
                w = jnp.exp((s - high) * scale)
                part = jnp.sum(w, axis=0, keepdims=True)
                if k > 0:
                    part = part + total[:, chunk] * shrink
                top[:, chunk] = high
                total[:, chunk] = part
                return w.astype(jnp.bfloat16), shrink

            def mix(chunk, w, shrink):
                mixed = jnp.dot(value, w, preferred_element_type=jnp.float32)
                if k > 0:
                    mixed = mixed + acc[:, chunk] * shrink
                acc[:, chunk] = mixed

            scored = [score(chunk) for chunk in todo[:2]]
            weighed = []
            for i, chunk in enumerate(todo):
                weighed.append(weigh(chunk, scored[i]))
                if i + 2 < len(todo):
                    scored.append(score(todo[i + 2]))
                if i > 0:
                    mix(todo[i - 1], *weighed[i - 1])
            mix(todo[-1], *weighed[-1])

    def finish(half):
        part = slice(half * half_rows, (half + 1) * half_rows)
        result = (acc[:, part] / total[:, part]).T.astype(jnp.bfloat16)
        leaving[2 * half:2 * half + 2] = result.reshape(2, per_group, tokens, HD)

    mine = pl.ds(chip * per_group, per_group)
    keep = pltpu.make_async_copy(leaving.at[1], done.at[mine], local_sems.at[4])

    def turn_rows(half):
        part = slice(half * half_rows, (half + 1) * half_rows)
        q_ext[:, part] = q_rows[part, :].T

    def send_half(half):
        if half == 0:
            result_home(0).start()
            keep.start()
        else:
            result_home(2).start()
            result_home(1).start()

    for which in (0, 1):
        for r in range(3):
            piece(which, r).start()
    prepare_bias()
    for r in (2, 0, 1):
        queries_out(r).start()
    column(0)
    local_copies[2].wait()
    prepare_rows(1, chip)
    queries_out(0).wait_recv()
    prepare_rows(0, y_chip)
    turn_rows(0)
    column(1)
    beside(0)
    attend(0, (0,))
    for r in (1, 2):
        queries_out(r).wait_recv()
        prepare_rows(slots[r], away[r])
    turn_rows(1)
    attend(0, (1,))

    @pl.when(z == 0)
    def _():
        finish(0)
        finish(1)
        send_half(1)
        send_half(0)

    for k in range(1, 4):
        if k == 1:
            column(2)
        beside(k)
        attend(k, (1, 0))

        @pl.when(z == k)
        def _():
            finish(1)
            send_half(1)
            finish(0)
            send_half(0)

        if k == 2:
            column(3)

    for which in (0, 1):
        for r in range(3):
            piece(which, r).wait_send()
    for r in range(3):
        queries_out(r).wait_send()
    for k in range(4):
        sent(k)
    keep.wait()
    for r in range(3):
        result_arrived(r)
    for place in range(H):
        out_ref[:, place * HD:(place + 1) * HD] = done[order_ref[place]]
    for r in range(3):
        result_home(r).wait_send()


def planes_local(queries, keys, values, block_index, block_count, head_order):
    tokens = queries.shape[0]
    planes = lax.axis_size("head")
    per_group = H // KVH
    rows = 4 * per_group * tokens
    table = block_index.transpose(0, 2, 1)
    any_spec = pl.BlockSpec(memory_space=pl.ANY)
    return pl.pallas_call(
        plane_kernel,
        out_shape=jax.ShapeDtypeStruct(queries.shape, jnp.bfloat16),
        in_specs=[any_spec] * 4 + [pl.BlockSpec(memory_space=pltpu.SMEM)],
        out_specs=pl.BlockSpec(memory_space=pltpu.VMEM),
        scratch_shapes=[
            pltpu.VMEM((planes * 2, 4 * tokens, HD), jnp.bfloat16),
            pltpu.VMEM((planes * 2, 4 * tokens, HD), jnp.bfloat16),
            pltpu.VMEM((4, tokens, per_group * HD), jnp.bfloat16),
            pltpu.VMEM((rows, 2 * HD), jnp.bfloat16),
            pltpu.VMEM((2 * HD, rows), jnp.bfloat16),
            pltpu.VMEM((HD, rows), jnp.float32),
            pltpu.VMEM((1, rows), jnp.float32),
            pltpu.VMEM((1, rows), jnp.float32),
            pltpu.VMEM((4,) + table.shape[1:], jnp.int32),
            pltpu.VMEM((HD, HD), jnp.float32),
            pltpu.VMEM((4, HD, HD), jnp.float32),
            pltpu.VMEM((H, tokens, HD), jnp.bfloat16),
            pltpu.VMEM((4, per_group, tokens, HD), jnp.bfloat16),
            pltpu.SemaphoreType.DMA((5,)),
            pltpu.SemaphoreType.DMA((2, 3)),
            pltpu.SemaphoreType.DMA((2, 3)),
            pltpu.SemaphoreType.DMA((2, 3)),
            pltpu.SemaphoreType.DMA((2, 3)),
            pltpu.SemaphoreType.DMA((planes, 4)),
            pltpu.SemaphoreType.DMA((planes, 2, 2)),
        ],
        compiler_params=pltpu.CompilerParams(
            collective_id=0, has_side_effects=True, vmem_limit_bytes=60 * 1024 * 1024
        ),
    )(queries, keys, values, table, head_order)


def solution(mesh):
    in_planes = mesh.shape["head"] == 4 and mesh.shape["ctx"] == 8
    return jax.shard_map(
        planes_local if in_planes else local,
        mesh=mesh,
        in_specs=(
            P(("head", "ctx"), None),
            P(("head", "ctx"), None),
            P(("head", "ctx"), None),
            P(),
            P(),
            P(),
        ),
        out_specs=P(("head", "ctx"), None),
        check_vma=False,
    )
```

```python
from functools import partial
import math

import jax
import jax.numpy as jnp
from jax import lax
from jax.experimental import pallas as pl
from jax.experimental.pallas import tpu as pltpu
from jax.sharding import PartitionSpec as P

H = 28
KVH = 4
HD = 128
BLOCK = 128


FLOOR = -1e30
MESH = pl.DeviceIdType.MESH


def positions(stripes, stripe_len, device, ctx_total):
    offsets = jnp.arange(stripes * stripe_len, dtype=jnp.int32)
    stripe = offsets // stripe_len
    return (stripe * ctx_total + device) * stripe_len + offsets % stripe_len


def keep_state(carried):
    return carried


def update_lanes(query_rows, key_lanes, value_lanes, allowed, score_scale, carried):
    running_max, running_sum, running_out = carried
    scores = (
        jnp.einsum("qgd,kgd->qgk", query_rows, key_lanes, preferred_element_type=jnp.float32)
        * score_scale
    )
    scores = jnp.where(allowed, scores, FLOOR)
    new_max = jnp.maximum(running_max, jnp.max(scores, axis=2))
    weights = jnp.where(allowed, jnp.exp(scores - new_max[:, :, None]), 0.0)
    factor = jnp.exp(running_max - new_max)
    new_sum = running_sum * factor + jnp.sum(weights, axis=2)
    update = jnp.einsum(
        "qgk,kgd->qgd",
        weights.astype(jnp.bfloat16),
        value_lanes,
        preferred_element_type=jnp.float32,
    )
    new_out = running_out * factor[:, :, None] + update
    return (new_max, new_sum, new_out)


def local(queries, keys, values, block_index, block_count, head_order):
    local_tokens = queries.shape[0]
    per_group = H // KVH
    head_total = lax.axis_size("head")
    ctx_total = lax.axis_size("ctx")
    ctx_here = lax.axis_index("ctx")
    head_here = lax.axis_index("head")
    query_split = queries.reshape(local_tokens, H, HD)
    key_split = keys.reshape(local_tokens, KVH, HD)
    value_split = values.reshape(local_tokens, KVH, HD)
    query_sorted = jnp.take(query_split, head_order, axis=1)
    kv_lists = (head_order // per_group).reshape(head_total, per_group)
    kv_pairs = jnp.stack([jnp.min(kv_lists, axis=1), jnp.max(kv_lists, axis=1)], axis=1).reshape(
        head_total * 2
    )
    key_sent = jnp.take(key_split, kv_pairs, axis=1).reshape(local_tokens, head_total, 2, HD)
    value_sent = jnp.take(value_split, kv_pairs, axis=1).reshape(local_tokens, head_total, 2, HD)
    own_heads = lax.dynamic_slice_in_dim(head_order, head_here * per_group, per_group)
    own_kv = own_heads // per_group
    slot_of = (own_kv == jnp.max(own_kv)).astype(jnp.int32)
    query_sent = query_sorted.reshape(local_tokens, head_total, per_group, HD)
    query_got, key_got, value_got = (
        lax.all_to_all(query_sent, "head", split_axis=1, concat_axis=0, tiled=True),
        lax.all_to_all(key_sent, "head", split_axis=1, concat_axis=0, tiled=True),
        lax.all_to_all(value_sent, "head", split_axis=1, concat_axis=0, tiled=True),
    )
    row_count = head_total * local_tokens
    slot_count = key_sent.shape[2]
    query_rows = query_got.reshape(row_count, per_group, HD)
    key_rows = key_got.reshape(row_count, slot_count, HD)
    value_rows = value_got.reshape(row_count, slot_count, HD)
    query_pos = positions(head_total, local_tokens, ctx_here, ctx_total)
    per_entry = min(local_tokens, BLOCK)
    entries = row_count // per_entry
    entry_blocks = query_pos[::per_entry] // BLOCK
    block_total = block_index.shape[2]
    block_iota = jnp.arange(block_total, dtype=jnp.int32)
    listed = jnp.take(jnp.take(block_index, entry_blocks, axis=0), own_heads, axis=1)
    counted = jnp.take(jnp.take(block_count, entry_blocks, axis=0), own_heads, axis=1)
    usable = block_iota[None, None, :] < counted[:, :, None]
    block_hits = (listed[:, :, :, None] == block_iota[None, None, None, :]) & usable[:, :, :, None]
    table_flags = jnp.any(block_hits, axis=2).astype(jnp.bfloat16)
    score_scale = 1.0 / math.sqrt(HD)
    initial = (
        jnp.full((row_count, per_group), FLOOR, jnp.float32),
        jnp.zeros((row_count, per_group), jnp.float32),
        jnp.zeros((row_count, per_group, HD), jnp.float32),
    )
    key_piece = lax.all_gather(key_rows, "ctx", axis=0, tiled=True)
    value_piece = lax.all_gather(value_rows, "ctx", axis=0, tiled=True)
    shard_total = key_piece.shape[0] // row_count

    def one_shard(number, inner_state):
        key_block = lax.dynamic_slice_in_dim(key_piece, number * row_count, row_count, 0)
        value_block = lax.dynamic_slice_in_dim(value_piece, number * row_count, row_count, 0)
        key_lanes = jnp.take(key_block, slot_of, axis=1)
        value_lanes = jnp.take(value_block, slot_of, axis=1)
        key_pos = positions(head_total, local_tokens, number, ctx_total)
        onehot = (block_iota[:, None] == (key_pos // BLOCK)[None, :]).astype(jnp.bfloat16)
        chosen = jnp.einsum("egb,bk->egk", table_flags, onehot, preferred_element_type=jnp.float32)
        spread = jnp.broadcast_to(
            chosen[:, None], (entries, per_entry, per_group, row_count)
        ).reshape(row_count, per_group, row_count)
        allowed = (spread > 0.5) & (key_pos[None, None, :] <= query_pos[:, None, None])
        return lax.cond(
            jnp.any(allowed),
            partial(update_lanes, query_rows, key_lanes, value_lanes, allowed, score_scale),
            keep_state,
            inner_state,
        )

    folded = lax.fori_loop(0, shard_total, one_shard, initial)
    running_max, running_sum, running_out = folded
    attended = (
        (running_out / running_sum[:, :, None])
        .astype(jnp.bfloat16)
        .reshape(row_count, 1, per_group, HD)
    )
    returned = lax.all_to_all(attended, "head", split_axis=0, concat_axis=1, tiled=True).reshape(
        local_tokens, H, HD
    )
    return returned.reshape(local_tokens, H * HD)


MASKED = -1e30


def plane_kernel(
    q_ref, k_ref, v_ref, table_ref, done,
    k_all, v_all, q_in, q_rows, q_ext, acc, top, total, lists, bias_by_block, bias_by_head,
    staying, leaving, local_sems, swap_send, swap_recv, send_sems, recv_sems,
):
    z = lax.axis_index("head")
    ctx = lax.axis_index("ctx")
    planes = lax.axis_size("head")
    tokens = q_ref.shape[0]
    per_group = H // KVH
    groups = KVH // 2
    heads = H // 2
    both = 2 * tokens
    rows = per_group * both
    half = groups * HD
    core = ctx % 2
    other = 1 - core
    chip = ctx // 2
    x_chip = chip + 1 - 2 * (chip % 2)
    y_chip = chip + 2 - 4 * (chip // 2)
    d_chip = x_chip + y_chip - chip
    sib = 2 * chip + other
    query_block = (z * 4 + chip) * both // BLOCK
    bufs = (k_all, v_all)
    heres = (k_ref, v_ref)

    def columns(which_core, width):
        return pl.ds(pl.multiple_of(which_core * width, width), width)

    def token_rows(which_core):
        return pl.ds(pl.multiple_of(which_core * tokens, tokens), tokens)

    local_copies = [
        pltpu.make_async_copy(
            q_ref.at[:, columns(core, heads * HD)], q_in.at[core], local_sems.at[0]
        ),
        pltpu.make_async_copy(table_ref.at[query_block], lists, local_sems.at[1]),
    ]
    for which in (0, 1):
        local_copies.append(pltpu.make_async_copy(
            heres[which].at[:, columns(core, half)],
            bufs[which].at[z * 4 + chip, token_rows(core)],
            local_sems.at[2 + which],
        ))
    for copy in local_copies:
        copy.start()

    barrier = pltpu.get_barrier_semaphore()

    def greet(head_to, ctx_to):
        pl.semaphore_signal(
            barrier, inc=1, device_id={"head": head_to, "ctx": ctx_to}, device_id_type=MESH
        )

    greet(z, sib)
    for which_core in (core, other):
        greet(z, 2 * x_chip + which_core)
        greet(z, 2 * y_chip + which_core)

    @pl.when(z > 0)
    def _():
        greet(z - 1, ctx)
        greet(z - 1, sib)

    @pl.when(z < planes - 1)
    def _():
        greet(z + 1, ctx)
        greet(z + 1, sib)

    pl.semaphore_wait(
        barrier, 5 + 2 * (z > 0).astype(jnp.int32) + 2 * (z < planes - 1).astype(jnp.int32)
    )

    def piece(which, to_core, kind, head_to, ctx_to):
        return pltpu.make_async_remote_copy(
            src_ref=heres[which].at[:, columns(to_core, half)],
            dst_ref=bufs[which].at[z * 4 + chip, token_rows(core)],
            send_sem=send_sems.at[0, kind],
            recv_sem=recv_sems.at[z, chip, which, core],
            device_id={"head": head_to, "ctx": ctx_to},
            device_id_type=MESH,
        )

    def whole(which, k, slot, kind, head_to, ctx_to):
        place = bufs[which].at[(z - k) * 4 + slot]
        return pltpu.make_async_remote_copy(
            src_ref=place,
            dst_ref=place,
            send_sem=send_sems.at[k, kind],
            recv_sem=recv_sems.at[z - k, slot, which, 0],
            device_id={"head": head_to, "ctx": ctx_to},
            device_id_type=MESH,
        )

    def piece_arrived(which, plane, slot, from_core):
        place = bufs[which].at[plane * 4 + slot, token_rows(from_core)]
        pltpu.make_async_remote_copy(
            src_ref=place,
            dst_ref=place,
            send_sem=send_sems.at[0, 0],
            recv_sem=recv_sems.at[plane, slot, which, from_core],
            device_id={"head": z, "ctx": sib},
            device_id_type=MESH,
        ).wait_recv()

    def whole_arrived(which, k, slot):
        whole(which, k, slot, 0, z, sib).wait_recv()

    def swap(src, dst, number):
        return pltpu.make_async_remote_copy(
            src_ref=src,
            dst_ref=dst,
            send_sem=swap_send.at[number],
            recv_sem=swap_recv.at[number],
            device_id={"head": z, "ctx": sib},
            device_id_type=MESH,
        )

    q_swap = swap(q_ref.at[:, columns(other, heads * HD)], q_in.at[core], 0)
    q_got = swap(q_in.at[other], q_in.at[other], 0)

    def own_pieces():
        for which in (0, 1):
            for cross, to_core in enumerate((core, other)):
                number = 2 * which + cross

                @pl.when(z < planes - 1)
                def _():
                    piece(which, to_core, number, z + 1, 2 * chip + to_core).start()

                piece(which, to_core, 4 + number, z, 2 * x_chip + to_core).start()
                piece(which, to_core, 8 + number, z, 2 * y_chip + to_core).start()
            piece(which, other, 12 + which, z, sib).start()

    def column(k):
        @pl.when(z >= k)
        def _():
            for which in (0, 1):
                if k == 1:
                    piece_arrived(which, z - 1, chip, core)
                    piece_arrived(which, z - 1, chip, other)
                else:
                    whole_arrived(which, k, chip)

                @pl.when(z < planes - 1)
                def _():
                    whole(which, k, chip, which, z + 1, ctx).start()

                whole(which, k, chip, 2 + which, z, 2 * x_chip + core).start()
                whole(which, k, chip, 4 + which, z, 2 * y_chip + core).start()

    def side_arrived(which, k, slot):
        if k == 0:
            piece_arrived(which, z, slot, core)
            piece_arrived(which, z, slot, other)
        else:
            whole_arrived(which, k, slot)

    def across(k):
        @pl.when(z >= k)
        def _():
            side_arrived(0, k, x_chip)
            whole(0, k, x_chip, 14, z, 2 * y_chip + core).start()
            side_arrived(1, k, y_chip)
            whole(1, k, y_chip, 15, z, 2 * x_chip + core).start()

    def rest(k):
        @pl.when(z >= k)
        def _():
            side_arrived(1, k, x_chip)
            side_arrived(0, k, y_chip)
            if k == 0:
                for which in (0, 1):
                    piece_arrived(which, z, chip, other)
            for which in (0, 1):
                whole_arrived(which, k, d_chip)

    def sent(k):
        @pl.when(z >= k)
        def _():
            if k == 0:
                @pl.when(z < planes - 1)
                def _():
                    for kind in range(4):
                        piece(0, core, kind, z, sib).wait_send()

                for kind in range(4, 14):
                    piece(0, core, kind, z, sib).wait_send()
            else:
                @pl.when(z < planes - 1)
                def _():
                    for kind in range(2):
                        whole(0, k, chip, kind, z, sib).wait_send()

                for kind in range(2, 6):
                    whole(0, k, chip, kind, z, sib).wait_send()
            for kind in (14, 15):
                whole(0, k, chip, kind, z, sib).wait_send()

    def prepare():
        for copy in local_copies:
            copy.wait()
        listed = lists[...]
        width = listed.shape[0]
        spot = lax.broadcasted_iota(jnp.int32, listed.shape, 0)
        last = jnp.min(jnp.where(listed == query_block, spot, width), axis=0, keepdims=True)
        listed = jnp.where(spot <= last, listed, -1)
        block = lax.broadcasted_iota(jnp.int32, (HD, H), 0)
        bias = jnp.full((HD, H), MASKED, jnp.float32)
        for e in range(width):
            bias = jnp.where(listed[e:e + 1, :] == block, 0.0, bias)
        bias_by_block[...] = jnp.zeros_like(bias_by_block)
        bias_by_block[:, :H] = bias
        bias_by_head[...] = bias_by_block[...].T
        q_got.wait_recv()
        for h in range(heads):
            group, row = h // per_group, (h % per_group) * both
            for part in (0, 1):
                start = row + part * tokens
                q_rows[group, start:start + tokens, :HD] = q_in[part, :, h * HD:(h + 1) * HD]
            q_rows[group, row:row + both, HD:] = jnp.broadcast_to(
                bias_by_head[pl.ds(core * heads + h, 1), :], (both, HD)
            ).astype(jnp.bfloat16)
        for group in range(groups):
            q_ext[group] = q_rows[group].T

    keys_here = 4 * both
    scale = 1.0 / math.sqrt(HD)
    chunks = [slice(i, min(i + 2 * HD, rows)) for i in range(0, rows, 2 * HD)]

    def attend(k, group):
        @pl.when(z >= k)
        def _():
            plane = z - k
            key_row = lax.broadcasted_iota(jnp.int32, (keys_here, HD), 0)
            key_lane = lax.broadcasted_iota(jnp.int32, (keys_here, HD), 1)
            block_of = (plane * keys_here + key_row) // BLOCK
            onehot = jnp.where(block_of == key_lane, 1.0, 0.0).astype(jnp.bfloat16)
            cols = slice(group * HD, (group + 1) * HD)
            key = k_all[pl.ds(plane * 4, 4), :, cols].reshape(keys_here, HD)
            value = v_all[pl.ds(plane * 4, 4), :, cols].reshape(keys_here, HD).T
            key = jnp.concatenate([key, onehot], axis=1)

            def score(chunk):
                return jnp.dot(key, q_ext[group, :, chunk], preferred_element_type=jnp.float32)

            def weigh(chunk, s):
                if k == 0:
                    row_pos = chip * both + lax.broadcasted_iota(jnp.int32, s.shape, 1) % both
                    key_pos = lax.broadcasted_iota(jnp.int32, s.shape, 0)
                    s = jnp.where(key_pos <= row_pos, s, MASKED)
                high = jnp.max(s, axis=0, keepdims=True)
                shrink = None
                if k > 0:
                    old = top[group, :, chunk]
                    high = jnp.maximum(high, old)
                    shrink = jnp.exp((old - high) * scale)
                w = jnp.exp((s - high) * scale)
                part = jnp.sum(w, axis=0, keepdims=True)
                if k > 0:
                    part = part + total[group, :, chunk] * shrink
                top[group, :, chunk] = high
                total[group, :, chunk] = part
                return w.astype(jnp.bfloat16), shrink

            def mix(chunk, w, shrink):
                mixed = jnp.dot(value, w, preferred_element_type=jnp.float32)
                if k > 0:
                    mixed = mixed + acc[group, :, chunk] * shrink
                acc[group, :, chunk] = mixed

            scored = [score(chunk) for chunk in chunks[:2]]
            weighed = []
            for i, chunk in enumerate(chunks):
                weighed.append(weigh(chunk, scored[i]))
                if i + 2 < len(chunks):
                    scored.append(score(chunks[i + 2]))
                if i > 0:
                    mix(chunks[i - 1], *weighed[i - 1])
            mix(chunks[-1], *weighed[-1])

    own_pieces()
    q_swap.start()
    prepare()
    across(0)
    column(1)
    rest(0)
    for k in range(4):
        attend(k, 0)
        if k < 3:
            across(k + 1)
        if k < 2:
            column(k + 2)
        attend(k, 1)
        if k < 3:
            rest(k + 1)

    mine = pl.ds(core * heads, heads)
    home = swap(leaving, done.at[mine], 1)
    for group in range(groups):
        result = (acc[group] / total[group]).T.astype(jnp.bfloat16)
        result = result.reshape(per_group, 2, tokens, HD)
        here = jnp.where(core == 0, result[:, 0], result[:, 1])
        there = jnp.where(core == 0, result[:, 1], result[:, 0])
        staying[group * per_group:(group + 1) * per_group] = here
        leaving[group * per_group:(group + 1) * per_group] = there
    home.start()
    keep = pltpu.make_async_copy(staying, done.at[mine], local_sems.at[4])
    keep.start()
    for k in range(4):
        sent(k)
    q_swap.wait_send()
    swap(leaving, done.at[pl.ds(other * heads, heads)], 1).wait_recv()
    keep.wait()
    home.wait_send()


def order_kernel(done, order_ref, out_ref, sems):
    copies = [
        pltpu.make_async_copy(
            done.at[order_ref[place]],
            out_ref.at[:, place * HD:(place + 1) * HD],
            sems.at[place],
        )
        for place in range(H)
    ]
    for copy in copies:
        copy.start()
    for copy in copies:
        copy.wait()


def planes_local(queries, keys, values, block_index, block_count, head_order):
    tokens = queries.shape[0]
    planes = lax.axis_size("head")
    rows = H // KVH * 2 * tokens
    groups = KVH // 2
    table = block_index.transpose(0, 2, 1)
    any_spec = pl.BlockSpec(memory_space=pl.ANY)
    attended = pl.pallas_call(
        plane_kernel,
        out_shape=jax.ShapeDtypeStruct((H, tokens, HD), jnp.bfloat16),
        in_specs=[any_spec] * 4,
        out_specs=any_spec,
        scratch_shapes=[
            pltpu.VMEM((planes * 4, 2 * tokens, groups * HD), jnp.bfloat16),
            pltpu.VMEM((planes * 4, 2 * tokens, groups * HD), jnp.bfloat16),
            pltpu.VMEM((2, tokens, H // 2 * HD), jnp.bfloat16),
            pltpu.VMEM((groups, rows, 2 * HD), jnp.bfloat16),
            pltpu.VMEM((groups, 2 * HD, rows), jnp.bfloat16),
            pltpu.VMEM((groups, HD, rows), jnp.float32),
            pltpu.VMEM((groups, 1, rows), jnp.float32),
            pltpu.VMEM((groups, 1, rows), jnp.float32),
            pltpu.VMEM(table.shape[1:], jnp.int32),
            pltpu.VMEM((HD, HD), jnp.float32),
            pltpu.VMEM((HD, HD), jnp.float32),
            pltpu.VMEM((H // 2, tokens, HD), jnp.bfloat16),
            pltpu.VMEM((H // 2, tokens, HD), jnp.bfloat16),
            pltpu.SemaphoreType.DMA((5,)),
            pltpu.SemaphoreType.DMA((2,)),
            pltpu.SemaphoreType.DMA((2,)),
            pltpu.SemaphoreType.DMA((planes, 16)),
            pltpu.SemaphoreType.DMA((planes, 4, 2, 2)),
        ],
        compiler_params=pltpu.CompilerParams(
            collective_id=0, has_side_effects=True, vmem_limit_bytes=60 * 1024 * 1024
        ),
    )(queries, keys, values, table)
    return pl.pallas_call(
        order_kernel,
        out_shape=jax.ShapeDtypeStruct(queries.shape, jnp.bfloat16),
        in_specs=[any_spec, pl.BlockSpec(memory_space=pltpu.SMEM)],
        out_specs=any_spec,
        scratch_shapes=[pltpu.SemaphoreType.DMA((H,))],
        compiler_params=pltpu.CompilerParams(vmem_limit_bytes=60 * 1024 * 1024),
    )(attended, head_order)


def solution(mesh):
    in_planes = mesh.shape["head"] == 4 and mesh.shape["ctx"] == 8
    return jax.shard_map(
        planes_local if in_planes else local,
        mesh=mesh,
        in_specs=(
            P(("head", "ctx"), None),
            P(("head", "ctx"), None),
            P(("head", "ctx"), None),
            P(),
            P(),
            P(),
        ),
        out_specs=P(("head", "ctx"), None),
        check_vma=False,
    )
```

```python
from functools import partial
import math

import jax
import jax.numpy as jnp
from jax import lax
from jax.experimental import pallas as pl
from jax.experimental.pallas import tpu as pltpu
from jax.sharding import PartitionSpec as P

H = 28
KVH = 4
HD = 128
BLOCK = 128


FLOOR = -1e30
MESH = pl.DeviceIdType.MESH


def positions(stripes, stripe_len, device, ctx_total):
    offsets = jnp.arange(stripes * stripe_len, dtype=jnp.int32)
    stripe = offsets // stripe_len
    return (stripe * ctx_total + device) * stripe_len + offsets % stripe_len


def keep_state(carried):
    return carried


def update_lanes(query_rows, key_lanes, value_lanes, allowed, score_scale, carried):
    running_max, running_sum, running_out = carried
    scores = (
        jnp.einsum("qgd,kgd->qgk", query_rows, key_lanes, preferred_element_type=jnp.float32)
        * score_scale
    )
    scores = jnp.where(allowed, scores, FLOOR)
    new_max = jnp.maximum(running_max, jnp.max(scores, axis=2))
    weights = jnp.where(allowed, jnp.exp(scores - new_max[:, :, None]), 0.0)
    factor = jnp.exp(running_max - new_max)
    new_sum = running_sum * factor + jnp.sum(weights, axis=2)
    update = jnp.einsum(
        "qgk,kgd->qgd",
        weights.astype(jnp.bfloat16),
        value_lanes,
        preferred_element_type=jnp.float32,
    )
    new_out = running_out * factor[:, :, None] + update
    return (new_max, new_sum, new_out)


def local(queries, keys, values, block_index, block_count, head_order):
    local_tokens = queries.shape[0]
    per_group = H // KVH
    head_total = lax.axis_size("head")
    ctx_total = lax.axis_size("ctx")
    ctx_here = lax.axis_index("ctx")
    head_here = lax.axis_index("head")
    query_split = queries.reshape(local_tokens, H, HD)
    key_split = keys.reshape(local_tokens, KVH, HD)
    value_split = values.reshape(local_tokens, KVH, HD)
    query_sorted = jnp.take(query_split, head_order, axis=1)
    kv_lists = (head_order // per_group).reshape(head_total, per_group)
    kv_pairs = jnp.stack([jnp.min(kv_lists, axis=1), jnp.max(kv_lists, axis=1)], axis=1).reshape(
        head_total * 2
    )
    key_sent = jnp.take(key_split, kv_pairs, axis=1).reshape(local_tokens, head_total, 2, HD)
    value_sent = jnp.take(value_split, kv_pairs, axis=1).reshape(local_tokens, head_total, 2, HD)
    own_heads = lax.dynamic_slice_in_dim(head_order, head_here * per_group, per_group)
    own_kv = own_heads // per_group
    slot_of = (own_kv == jnp.max(own_kv)).astype(jnp.int32)
    query_sent = query_sorted.reshape(local_tokens, head_total, per_group, HD)
    query_got, key_got, value_got = (
        lax.all_to_all(query_sent, "head", split_axis=1, concat_axis=0, tiled=True),
        lax.all_to_all(key_sent, "head", split_axis=1, concat_axis=0, tiled=True),
        lax.all_to_all(value_sent, "head", split_axis=1, concat_axis=0, tiled=True),
    )
    row_count = head_total * local_tokens
    slot_count = key_sent.shape[2]
    query_rows = query_got.reshape(row_count, per_group, HD)
    key_rows = key_got.reshape(row_count, slot_count, HD)
    value_rows = value_got.reshape(row_count, slot_count, HD)
    query_pos = positions(head_total, local_tokens, ctx_here, ctx_total)
    per_entry = min(local_tokens, BLOCK)
    entries = row_count // per_entry
    entry_blocks = query_pos[::per_entry] // BLOCK
    block_total = block_index.shape[2]
    block_iota = jnp.arange(block_total, dtype=jnp.int32)
    listed = jnp.take(jnp.take(block_index, entry_blocks, axis=0), own_heads, axis=1)
    counted = jnp.take(jnp.take(block_count, entry_blocks, axis=0), own_heads, axis=1)
    usable = block_iota[None, None, :] < counted[:, :, None]
    block_hits = (listed[:, :, :, None] == block_iota[None, None, None, :]) & usable[:, :, :, None]
    table_flags = jnp.any(block_hits, axis=2).astype(jnp.bfloat16)
    score_scale = 1.0 / math.sqrt(HD)
    initial = (
        jnp.full((row_count, per_group), FLOOR, jnp.float32),
        jnp.zeros((row_count, per_group), jnp.float32),
        jnp.zeros((row_count, per_group, HD), jnp.float32),
    )
    key_piece = lax.all_gather(key_rows, "ctx", axis=0, tiled=True)
    value_piece = lax.all_gather(value_rows, "ctx", axis=0, tiled=True)
    shard_total = key_piece.shape[0] // row_count

    def one_shard(number, inner_state):
        key_block = lax.dynamic_slice_in_dim(key_piece, number * row_count, row_count, 0)
        value_block = lax.dynamic_slice_in_dim(value_piece, number * row_count, row_count, 0)
        key_lanes = jnp.take(key_block, slot_of, axis=1)
        value_lanes = jnp.take(value_block, slot_of, axis=1)
        key_pos = positions(head_total, local_tokens, number, ctx_total)
        onehot = (block_iota[:, None] == (key_pos // BLOCK)[None, :]).astype(jnp.bfloat16)
        chosen = jnp.einsum("egb,bk->egk", table_flags, onehot, preferred_element_type=jnp.float32)
        spread = jnp.broadcast_to(
            chosen[:, None], (entries, per_entry, per_group, row_count)
        ).reshape(row_count, per_group, row_count)
        allowed = (spread > 0.5) & (key_pos[None, None, :] <= query_pos[:, None, None])
        return lax.cond(
            jnp.any(allowed),
            partial(update_lanes, query_rows, key_lanes, value_lanes, allowed, score_scale),
            keep_state,
            inner_state,
        )

    folded = lax.fori_loop(0, shard_total, one_shard, initial)
    running_max, running_sum, running_out = folded
    attended = (
        (running_out / running_sum[:, :, None])
        .astype(jnp.bfloat16)
        .reshape(row_count, 1, per_group, HD)
    )
    returned = lax.all_to_all(attended, "head", split_axis=0, concat_axis=1, tiled=True).reshape(
        local_tokens, H, HD
    )
    return returned.reshape(local_tokens, H * HD)


MASKED = -1e30


def plane_kernel(
    q_ref, k_ref, v_ref, table_ref, done,
    k_all, v_all, q_in, q_rows, q_ext, acc, top, total, lists, bias_by_block,
    bias_by_head, leaving, local_sems, piece_send, piece_recv, head_send, head_recv,
    send_sems, recv_sems,
):
    z = lax.axis_index("head")
    ctx = lax.axis_index("ctx")
    planes = lax.axis_size("head")
    tokens = q_ref.shape[0]
    per_group = H // KVH
    width = per_group * HD
    rows = 4 * per_group * tokens
    lane_keys = 4 * tokens
    core = ctx % 2
    other = 1 - core
    chip = ctx // 2
    x_chip = chip + 1 - 2 * (chip % 2)
    y_chip = chip + 2 - 4 * (chip // 2)
    d_chip = x_chip + y_chip - chip
    away = (y_chip, x_chip, d_chip)
    slots = (0, 2, 3)
    sib = 2 * chip + other
    bufs = (k_all, v_all)
    heres = (k_ref, v_ref)

    def head_columns(of_chip, size):
        return pl.ds(pl.multiple_of(of_chip * size, size), size)

    def chip_rows(of_chip):
        return pl.ds(pl.multiple_of(of_chip * tokens, tokens), tokens)

    own_places = [bufs[which].at[z * 2 + core, chip_rows(chip)] for which in (0, 1)]
    local_copies = [
        pltpu.make_async_copy(
            heres[which].at[:, head_columns(chip, HD)], own_places[which], local_sems.at[which]
        )
        for which in (0, 1)
    ]
    local_copies.append(pltpu.make_async_copy(
        q_ref.at[:, head_columns(chip, width)], q_in.at[1], local_sems.at[2]
    ))
    local_copies.append(pltpu.make_async_copy(
        table_ref.at[pl.ds(z * 4, 4)], lists, local_sems.at[3]
    ))
    for copy in local_copies:
        copy.start()

    barrier = pltpu.get_barrier_semaphore()

    def greet(head_to, ctx_to):
        pl.semaphore_signal(
            barrier, inc=1, device_id={"head": head_to, "ctx": ctx_to}, device_id_type=MESH
        )

    greet(z, sib)
    for near in away:
        greet(z, 2 * near + core)

    @pl.when(z > 0)
    def _():
        greet(z - 1, ctx)

    @pl.when(z < planes - 1)
    def _():
        greet(z + 1, ctx)

    pl.semaphore_wait(
        barrier, 4 + (z > 0).astype(jnp.int32) + (z < planes - 1).astype(jnp.int32)
    )

    def remote(src, dst, send_sem, recv_sem, head_to, ctx_to):
        return pltpu.make_async_remote_copy(
            src_ref=src,
            dst_ref=dst,
            send_sem=send_sem,
            recv_sem=recv_sem,
            device_id={"head": head_to, "ctx": ctx_to},
            device_id_type=MESH,
        )

    def piece(which, r):
        return remote(
            heres[which].at[:, head_columns(away[r], HD)],
            own_places[which],
            piece_send.at[which, r],
            piece_recv.at[which, r],
            z, 2 * away[r] + core,
        )

    def piece_arrived(which, r):
        place = bufs[which].at[z * 2 + core, chip_rows(away[r])]
        remote(
            place, place, piece_send.at[which, r], piece_recv.at[which, r], z, sib
        ).wait_recv()

    def queries_out(r):
        return remote(
            q_ref.at[:, head_columns(away[r], width)],
            q_in.at[slots[r]],
            head_send.at[0, r],
            head_recv.at[0, r],
            z, 2 * away[r] + core,
        )

    def result_home(r):
        return remote(
            leaving.at[slots[r]],
            done.at[pl.ds(chip * per_group, per_group)],
            head_send.at[1, r],
            head_recv.at[1, r],
            z, 2 * away[r] + core,
        )

    def result_arrived(r):
        remote(
            leaving.at[slots[r]],
            done.at[pl.ds(away[r] * per_group, per_group)],
            head_send.at[1, r],
            head_recv.at[1, r],
            z, sib,
        ).wait_recv()

    def whole(which, k, lane, kind, head_to, ctx_to):
        place = bufs[which].at[(z - k) * 2 + lane]
        return remote(
            place, place, send_sems.at[k, kind], recv_sems.at[z - k, lane, which],
            head_to, ctx_to,
        )

    def column(k):
        @pl.when(z >= k)
        def _():
            for which in (0, 1):
                if k == 0:
                    local_copies[which].wait()
                    for r in range(3):
                        piece_arrived(which, r)
                else:
                    whole(which, k, core, 0, z, sib).wait_recv()

                @pl.when(z < planes - 1)
                def _():
                    whole(which, k, core, which, z + 1, ctx).start()

                whole(which, k, core, 2 + which, z, sib).start()

    def beside(k):
        @pl.when(z >= k)
        def _():
            for which in (0, 1):
                whole(which, k, other, 0, z, sib).wait_recv()

    def sent(k):
        @pl.when(z >= k)
        def _():
            @pl.when(z < planes - 1)
            def _():
                for kind in (0, 1):
                    whole(0, k, core, kind, z, sib).wait_send()

            for kind in (2, 3):
                whole(0, k, core, kind, z, sib).wait_send()

    def prepare_bias():
        local_copies[3].wait()
        listed = lists[...]
        entries = listed.shape[1]
        spot = lax.broadcasted_iota(jnp.int32, listed.shape, 1)
        query_block = z * 4 + lax.broadcasted_iota(jnp.int32, listed.shape, 0)
        last = jnp.min(jnp.where(listed == query_block, spot, entries), axis=1, keepdims=True)
        listed = jnp.where(spot <= last, listed, -1)
        bias_by_block[...] = jnp.zeros_like(bias_by_block)
        for chip_here in range(4):
            block = lax.broadcasted_iota(jnp.int32, (entries, H), 0)
            bias = jnp.full((entries, H), MASKED, jnp.float32)
            for e in range(entries):
                bias = jnp.where(listed[chip_here, e:e + 1, :] == block, 0.0, bias)
            bias_by_block[:entries, :H] = bias
            bias_by_head[chip_here] = bias_by_block[...].T

    def prepare_rows(r, of_chip):
        for g in range(per_group):
            row = (r * per_group + g) * tokens
            q_rows[row:row + tokens, :HD] = q_in[r, :, g * HD:(g + 1) * HD]
            q_rows[row:row + tokens, HD:] = jnp.broadcast_to(
                bias_by_head[of_chip, pl.ds(chip * per_group + g, 1), :], (tokens, HD)
            ).astype(jnp.bfloat16)

    keys_here = 2 * lane_keys
    half_rows = rows // 2
    scale = 1.0 / math.sqrt(HD)
    starts = range(0, half_rows, 2 * HD)
    chunks = [
        [slice(h * half_rows + i, h * half_rows + min(i + 2 * HD, half_rows)) for i in starts]
        for h in (0, 1)
    ]

    def attend(k, halves):
        @pl.when(z >= k)
        def _():
            plane = z - k
            key_row = lax.broadcasted_iota(jnp.int32, (keys_here, HD), 0)
            key_lane = lax.broadcasted_iota(jnp.int32, (keys_here, HD), 1)
            block_of = plane * 4 + key_row % lane_keys // tokens
            onehot = jnp.where(block_of == key_lane, 1.0, 0.0).astype(jnp.bfloat16)
            key = k_all[pl.ds(plane * 2, 2)].reshape(keys_here, HD)
            value = v_all[pl.ds(plane * 2, 2)].reshape(keys_here, HD).T
            key = jnp.concatenate([key, onehot], axis=1)
            todo = [chunk for half in halves for chunk in chunks[half]]

            def score(chunk):
                return jnp.dot(key, q_ext[:, chunk], preferred_element_type=jnp.float32)

            def weigh(chunk, s):
                if k == 0:
                    key_at = lax.broadcasted_iota(jnp.int32, (keys_here, 1), 0)
                    key_pos = (
                        key_at % lane_keys // tokens * 2 + key_at // lane_keys
                    ) * tokens + key_at % tokens
                    row_at = chunk.start + lax.broadcasted_iota(
                        jnp.int32, (1, chunk.stop - chunk.start), 1
                    )
                    source = row_at // (per_group * tokens)
                    row_chip = jnp.where(
                        source == 0, y_chip,
                        jnp.where(source == 1, chip, jnp.where(source == 2, x_chip, d_chip)),
                    )
                    row_pos = (row_chip * 2 + core) * tokens + row_at % tokens
                    s = jnp.where(key_pos <= row_pos, s, MASKED)
                high = jnp.max(s, axis=0, keepdims=True)
                shrink = None
                if k > 0:
                    old = top[:, chunk]
                    high = jnp.maximum(high, old)
                    shrink = jnp.exp((old - high) * scale)
                w = jnp.exp((s - high) * scale)
                part = jnp.sum(w, axis=0, keepdims=True)
                if k > 0:
                    part = part + total[:, chunk] * shrink
                top[:, chunk] = high
                total[:, chunk] = part
                return w.astype(jnp.bfloat16), shrink

            def mix(chunk, w, shrink):
                mixed = jnp.dot(value, w, preferred_element_type=jnp.float32)
                if k > 0:
                    mixed = mixed + acc[:, chunk] * shrink
                acc[:, chunk] = mixed

            scored = [score(chunk) for chunk in todo[:2]]
            weighed = []
            for i, chunk in enumerate(todo):
                weighed.append(weigh(chunk, scored[i]))
                if i + 2 < len(todo):
                    scored.append(score(todo[i + 2]))
                if i > 0:
                    mix(todo[i - 1], *weighed[i - 1])
            mix(todo[-1], *weighed[-1])

    def finish(half):
        part = slice(half * half_rows, (half + 1) * half_rows)
        result = (acc[:, part] / total[:, part]).T.astype(jnp.bfloat16)
        leaving[2 * half:2 * half + 2] = result.reshape(2, per_group, tokens, HD)

    mine = pl.ds(chip * per_group, per_group)
    keep = pltpu.make_async_copy(leaving.at[1], done.at[mine], local_sems.at[4])

    def turn_rows(half):
        part = slice(half * half_rows, (half + 1) * half_rows)
        q_ext[:, part] = q_rows[part, :].T

    def send_half(half):
        if half == 0:
            result_home(0).start()
            keep.start()
        else:
            result_home(2).start()
            result_home(1).start()

    for which in (0, 1):
        for r in range(3):
            piece(which, r).start()
    prepare_bias()
    for r in (2, 0, 1):
        queries_out(r).start()
    column(0)
    local_copies[2].wait()
    prepare_rows(1, chip)
    queries_out(0).wait_recv()
    prepare_rows(0, y_chip)
    turn_rows(0)
    column(1)
    beside(0)
    attend(0, (0,))
    for r in (1, 2):
        queries_out(r).wait_recv()
        prepare_rows(slots[r], away[r])
    turn_rows(1)
    attend(0, (1,))

    @pl.when(z == 0)
    def _():
        finish(0)
        finish(1)
        send_half(1)
        send_half(0)

    for k in range(1, 4):
        if k == 1:
            column(2)
        beside(k)
        if k < 3:
            attend(k, (1, 0))
        else:
            attend(k, (1,))

        @pl.when(z == k)
        def _():
            finish(1)
            send_half(1)

        if k == 3:
            attend(k, (0,))

        @pl.when(z == k)
        def _():
            finish(0)
            send_half(0)

        if k == 2:
            column(3)

    for which in (0, 1):
        for r in range(3):
            piece(which, r).wait_send()
    for r in range(3):
        queries_out(r).wait_send()
    for k in range(4):
        sent(k)
    keep.wait()
    for r in range(3):
        result_arrived(r)
    for r in range(3):
        result_home(r).wait_send()


def order_kernel(done, order_ref, out_ref):
    for place in range(H):
        out_ref[:, place * HD:(place + 1) * HD] = done[order_ref[place]]


def planes_local(queries, keys, values, block_index, block_count, head_order):
    tokens = queries.shape[0]
    planes = lax.axis_size("head")
    per_group = H // KVH
    rows = 4 * per_group * tokens
    table = block_index.transpose(0, 2, 1)
    any_spec = pl.BlockSpec(memory_space=pl.ANY)
    attended = pl.pallas_call(
        plane_kernel,
        out_shape=jax.ShapeDtypeStruct((H, tokens, HD), jnp.bfloat16),
        in_specs=[any_spec] * 4,
        out_specs=any_spec,
        scratch_shapes=[
            pltpu.VMEM((planes * 2, 4 * tokens, HD), jnp.bfloat16),
            pltpu.VMEM((planes * 2, 4 * tokens, HD), jnp.bfloat16),
            pltpu.VMEM((4, tokens, per_group * HD), jnp.bfloat16),
            pltpu.VMEM((rows, 2 * HD), jnp.bfloat16),
            pltpu.VMEM((2 * HD, rows), jnp.bfloat16),
            pltpu.VMEM((HD, rows), jnp.float32),
            pltpu.VMEM((1, rows), jnp.float32),
            pltpu.VMEM((1, rows), jnp.float32),
            pltpu.VMEM((4,) + table.shape[1:], jnp.int32),
            pltpu.VMEM((HD, HD), jnp.float32),
            pltpu.VMEM((4, HD, HD), jnp.float32),
            pltpu.VMEM((4, per_group, tokens, HD), jnp.bfloat16),
            pltpu.SemaphoreType.DMA((5,)),
            pltpu.SemaphoreType.DMA((2, 3)),
            pltpu.SemaphoreType.DMA((2, 3)),
            pltpu.SemaphoreType.DMA((2, 3)),
            pltpu.SemaphoreType.DMA((2, 3)),
            pltpu.SemaphoreType.DMA((planes, 4)),
            pltpu.SemaphoreType.DMA((planes, 2, 2)),
        ],
        compiler_params=pltpu.CompilerParams(
            collective_id=0, has_side_effects=True, vmem_limit_bytes=60 * 1024 * 1024
        ),
    )(queries, keys, values, table)
    return pl.pallas_call(
        order_kernel,
        out_shape=jax.ShapeDtypeStruct(queries.shape, jnp.bfloat16),
        in_specs=[
            pl.BlockSpec(memory_space=pltpu.VMEM), pl.BlockSpec(memory_space=pltpu.SMEM)
        ],
        out_specs=pl.BlockSpec(memory_space=pltpu.VMEM),
        compiler_params=pltpu.CompilerParams(vmem_limit_bytes=60 * 1024 * 1024),
    )(attended, head_order)


def solution(mesh):
    in_planes = mesh.shape["head"] == 4 and mesh.shape["ctx"] == 8
    return jax.shard_map(
        planes_local if in_planes else local,
        mesh=mesh,
        in_specs=(
            P(("head", "ctx"), None),
            P(("head", "ctx"), None),
            P(("head", "ctx"), None),
            P(),
            P(),
            P(),
        ),
        out_specs=P(("head", "ctx"), None),
        check_vma=False,
    )
```
